256 devices in a mesh: section: 16 (over x, y), coal: 16 (over z, core).
Axes of the slice: x: 4, y: 4, z: 8, core: 2. Of those that a mesh axis runs over, the one named last changes fastest.
Arguments:
- base_rows: bfloat16 [4, 4608], replicated, may hold values from -6 to 6
- group_out: bfloat16 [10, 4, 4608], replicated, may hold values from -3 to 3
- pre_gain: float32 [16, 4608], P('section'), may hold values from 0.5 to 1.5
- w_query: bfloat16 [16, 4608, 256], P('section'), may hold values from -0.09375 to 0.09375
- w_key: bfloat16 [16, 4608, 128], P('section'), may hold values from -0.09375 to 0.09375
- w_value: bfloat16 [16, 4608, 128], P('section'), may hold values from -0.09375 to 0.09375
- w_out: bfloat16 [16, 256, 4608], P('section'), may hold values from -0.375 to 0.375
- post_gain: float32 [16, 4608], P('section'), may hold values from 0.5 to 1.5
- key_cache: bfloat16 [16, 2048, 128], P('section'), may hold values from -6 to 6
- value_cache: bfloat16 [16, 2048, 128], P('section'), may hold values from -6 to 6
- final_gain: float32 [4608], replicated, may hold values from 0.5 to 1.5
- answer_rows: bfloat16 [4096, 4608], P('section'), may hold values from -0.25 to 0.25
Outputs:
- interactions: float32 [1024, 4, 4096], P('coal', None, 'section')
- shapley: float32 [10, 4, 4096], P(None, None, 'section')
The draws below stay inside these ranges and needn't reach their ends.
All inputs are finite; a program needn't handle non-finite values.
Results may differ from the reference program's by a relative error of at most 0.0013.
Values sent between devices are 32-bit elements; how exact they have to be, the bound alone decides.
A program may use at most 128 MiB of HBM per device.

```python
import jax
import jax.numpy as jnp
from jax import lax

D = 4608
HEAD_DIM = 128
QHEADS = 2
GROUPS = 10
SEQ = 4
PREFIX = 2048
CANDS = 4096
COALS = 1024
N_SECTION = 16


def block_levels(key, extent, pieces, least, top_value):
    def one(axis_at, blocks):
        heights = jax.random.uniform(jax.random.fold_in(jax.random.fold_in(key, 6), axis_at), (blocks,), jnp.float32, least / len(pieces), top_value / len(pieces))
        return jnp.repeat(jnp.exp(heights), extent[axis_at] // blocks).reshape((-1,) + (1,) * (len(extent) - axis_at - 1))

    gain = one(*pieces[0])
    for cut in pieces[1:]:
        gain = gain * one(*cut)
    return gain


def scatter_about(stream_key, dims, width, bound, split=(), kind=jnp.bfloat16):
    entries = jax.random.normal(stream_key, dims, jnp.float32) * width
    if len(split) > 0:
        entries = block_levels(stream_key, dims, split, -0.22, 0.18) * entries
    return jnp.clip(entries, min=-bound, max=bound).astype(kind)


def setup_inputs(seed: int = 0) -> dict:
    key_list = jax.random.split(jax.random.key(seed), 13)
    return {
        "base_rows": scatter_about(key_list[0], (SEQ, D), 1.0, 6.0),
        "group_out": scatter_about(key_list[1], (GROUPS, SEQ, D), 0.5, 3.0),
        "pre_gain": jnp.clip(1.0 + 0.1 * jax.random.normal(key_list[2], (N_SECTION, D), jnp.float32), 0.5, 1.5),
        "w_query": scatter_about(key_list[3], (N_SECTION, D, QHEADS * HEAD_DIM), D ** -0.5, 0.09375, ((0, 16),)),
        "w_key": scatter_about(key_list[4], (N_SECTION, D, HEAD_DIM), D ** -0.5, 0.09375, ((0, 16),)),
        "w_value": scatter_about(key_list[5], (N_SECTION, D, HEAD_DIM), D ** -0.5, 0.09375, ((0, 16),)),
        "w_out": scatter_about(key_list[6], (N_SECTION, QHEADS * HEAD_DIM, D), (QHEADS * HEAD_DIM) ** -0.5, 0.375, ((0, 16),)),
        "post_gain": jnp.clip(1.0 + 0.1 * jax.random.normal(key_list[7], (N_SECTION, D), jnp.float32), 0.5, 1.5),
        "key_cache": scatter_about(key_list[8], (N_SECTION, PREFIX, HEAD_DIM), 1.0, 6.0, ((0, 16),)),
        "value_cache": scatter_about(key_list[9], (N_SECTION, PREFIX, HEAD_DIM), 1.0, 6.0, ((0, 16),)),
        "final_gain": jnp.clip(1.0 + 0.1 * jax.random.normal(key_list[10], (D,), jnp.float32), 0.5, 1.5),
        "answer_rows": scatter_about(key_list[11], (CANDS, D), (D // 9) ** -0.5, 0.25, ((0, 16),)),
    }


norm_eps = 1e-06
attn_cap = 50.0
logit_cap = 30.0
query_scale = 1.0 / 12.0
highest = lax.Precision.HIGHEST

def matmul(left, right):
    return jnp.dot(left.astype(jnp.float32), right.astype(jnp.float32), precision=highest)

def rms_scale(values, gain_row):
    return values * lax.rsqrt(lax.optimization_barrier(jnp.mean(values * values, axis=-1, keepdims=True)) + norm_eps) * gain_row

def rotary(values, cosine, sine_table):
    half_dim = values.shape[-1] // 2
    front_half = values[..., :half_dim]
    second = values[..., half_dim:]
    return jnp.concatenate([front_half * cosine - second * sine_table, second * cosine + front_half * sine_table], axis=-1)

def rope_tables(prefix_len, seq_len, head_dim):
    half_dim = head_dim // 2
    places = prefix_len + jnp.arange(seq_len, dtype=jnp.float32)
    inverse = 10000.0 ** (-2.0 * jnp.arange(half_dim, dtype=jnp.float32) / head_dim)
    angles = places[:, None] * inverse[None, :]
    return (jnp.cos(angles), jnp.sin(angles))

def attend(hidden, pre_gain_row, w_query, w_key, w_value, w_out, post_gain_row, key_cache, value_cache, seq_len):
    total_rows = hidden.shape[0]
    head_dim = key_cache.shape[1]
    q_heads = w_query.shape[1] // head_dim
    groups_in = total_rows // seq_len
    normed = rms_scale(hidden, pre_gain_row)
    queries = matmul(normed, w_query).reshape(groups_in, seq_len, q_heads, head_dim)
    key_new = matmul(normed, w_key).reshape(groups_in, seq_len, head_dim)
    value_new = matmul(normed, w_value).reshape(groups_in, seq_len, head_dim)
    cosine, sine_table = rope_tables(key_cache.shape[0], seq_len, head_dim)
    queries = rotary(queries, cosine[:, None, :], sine_table[:, None, :])
    key_new = rotary(key_new, cosine, sine_table)
    keys_old = key_cache.astype(jnp.float32)
    values_old = value_cache.astype(jnp.float32)
    past_scores = jnp.einsum('cshd,pd->cshp', queries, keys_old, precision=highest) * query_scale
    recent = jnp.einsum('cshd,ctd->csht', queries, key_new, precision=highest) * query_scale
    causal = jnp.arange(seq_len)[:, None] >= jnp.arange(seq_len)[None, :]
    past_exp = jnp.exp(attn_cap * jnp.tanh(past_scores / attn_cap))
    recent_exp = jnp.where(causal[None, :, None, :], jnp.exp(attn_cap * jnp.tanh(recent / attn_cap)), 0.0)
    totals = lax.optimization_barrier(jnp.sum(past_exp, axis=-1, keepdims=True)) + lax.optimization_barrier(jnp.sum(recent_exp, axis=-1, keepdims=True))
    past_weights = past_exp / totals
    recent_weights = recent_exp / totals
    attended = jnp.einsum('cshp,pd->cshd', past_weights, values_old, precision=highest)
    attended = attended + jnp.einsum('csht,ctd->cshd', recent_weights, value_new, precision=highest)
    attended = attended.reshape(total_rows, q_heads * head_dim)
    projected = matmul(attended, w_out)
    return hidden + rms_scale(projected, post_gain_row)

def moebius(coeffs, bit_count):
    total_rows = coeffs.shape[0]
    for bit_idx in range(bit_count):
        stride = 1 << bit_idx
        blocks = coeffs.reshape(total_rows // (2 * stride), 2, stride, -1)
        coeffs = jnp.concatenate([blocks[:, :1], blocks[:, 1:] - blocks[:, :1]], axis=1).reshape(total_rows, -1)
    return coeffs

def shapley_weights(first_id, id_count, groups):
    id_list = first_id + jnp.arange(id_count, dtype=jnp.int32)
    member = (id_list[:, None] >> jnp.arange(groups, dtype=jnp.int32)[None, :] & 1).astype(jnp.float32)
    set_sizes = jnp.maximum(lax.optimization_barrier(jnp.sum(member, axis=1, keepdims=True)), 1.0)
    return member / set_sizes

def reference(base_rows, group_out, pre_gain, w_query, w_key, w_value, w_out, post_gain, key_cache, value_cache, final_gain, answer_rows):
    id_list = jnp.arange(COALS, dtype=jnp.int32)
    member = (id_list[:, None] >> jnp.arange(GROUPS, dtype=jnp.int32)[None, :] & 1).astype(jnp.float32)
    mixture = matmul(member, group_out.reshape(GROUPS, SEQ * D))
    mixture = mixture + base_rows.reshape(1, SEQ * D).astype(jnp.float32)
    hidden = mixture.reshape(COALS * SEQ, D)
    for layer_idx in range(N_SECTION):
        hidden = attend(hidden, pre_gain[layer_idx], w_query[layer_idx], w_key[layer_idx], w_value[layer_idx], w_out[layer_idx], post_gain[layer_idx], key_cache[layer_idx], value_cache[layer_idx], SEQ)
    normed = rms_scale(hidden, final_gain)
    logits = jnp.einsum('nd,kd->nk', normed, answer_rows.astype(jnp.float32), precision=highest)
    capped = logit_cap * jnp.tanh(logits / logit_cap)
    log_probs = capped - jnp.log(lax.optimization_barrier(jnp.sum(jnp.exp(capped), axis=-1)))[:, None]
    ordered = log_probs.reshape(COALS, SEQ * CANDS)
    coeffs = moebius(ordered, GROUPS)
    weights = shapley_weights(0, COALS, GROUPS)
    shapley = jnp.einsum('cg,cn->gn', weights, coeffs, precision=highest)
    return (coeffs.reshape(COALS, SEQ, CANDS), shapley.reshape(GROUPS, SEQ, CANDS))
```

```python
import functools

import jax
import jax.numpy as jnp
import numpy as np
from jax import lax
from jax.experimental import pallas as pl
from jax.experimental.pallas import tpu as pltpu
from jax.sharding import PartitionSpec as P

f32, bf16 = jnp.float32, jnp.bfloat16
MESH = pl.DeviceIdType.MESH

D = 4608
HEAD = 128
PREFIX = 2048
GROUPS = 10
SECTIONS = 16
COALS = 16
R = 8
M = 32
CANDS = 256
EPS = 1e-6
LAST = SECTIONS - 1
MAX_LAG = 2 * LAST + 2 * 5 + 2


def rope_rows():
    half = HEAD // 2
    places = PREFIX + np.arange(R) % 4
    inverse = 10000.0 ** (-2.0 * np.arange(half) / HEAD)
    angles = places[:, None] * inverse[None, :]
    cosine, sine = np.cos(angles), np.sin(angles)
    return (
        np.concatenate([cosine, cosine], axis=1).astype(np.float32),
        np.concatenate([-sine, sine], axis=1).astype(np.float32),
    )


def split2(x):
    high = x.astype(bf16).astype(f32)
    return jnp.concatenate([high, x - high], axis=0).astype(bf16)


def fold(y):
    half = y.shape[0] // 2
    return y[:half] + y[half:]


def dot(left, right):
    return jnp.dot(left, right, preferred_element_type=f32)


def block(x, w_ref, wo_ref, kt_ref, v_ref, pre, post, cosine, sine):
    rows = x.shape[0]
    inv = lax.rsqrt(jnp.mean(x * x, axis=-1, keepdims=True) + EPS)
    y = fold(dot(split2(x * pre), w_ref[...])) * inv

    def rotated(z):
        return z * cosine + pltpu.roll(z, HEAD // 2, 1) * sine

    q = jnp.concatenate([rotated(y[:, :128]), rotated(y[:, 128:256])], axis=0)
    q = q * (1.0 / 600.0)
    k = rotated(y[:, 256:384])
    v = y[:, 384:512]
    p = jnp.exp(50.0 * jnp.tanh(fold(dot(split2(q), kt_ref[...]))))
    mixed = fold(dot(split2(p), v_ref[...]))
    total = jnp.sum(p, axis=-1, keepdims=True)
    place = lax.broadcasted_iota(jnp.int32, (2 * rows, 1), 0) % 4
    for back in range(4):
        k_back = pltpu.roll(k, back, 0) if back else k
        v_back = pltpu.roll(v, back, 0) if back else v
        score = jnp.sum(
            q * jnp.concatenate([k_back, k_back], axis=0), axis=-1, keepdims=True
        )
        weight = jnp.where(place >= back, jnp.exp(50.0 * jnp.tanh(score)), 0.0)
        total = total + weight
        mixed = mixed + weight * jnp.concatenate([v_back, v_back], axis=0)
    attended = mixed / total
    attended = jnp.concatenate([attended[:rows], attended[rows:]], axis=1)
    proj = fold(dot(split2(attended), wo_ref[...]))
    scale = lax.rsqrt(jnp.mean(proj * proj, axis=-1, keepdims=True) + EPS)
    return x + proj * scale * post


def shapley_weights(first_id):
    shape = (16 * 8, 256)
    row = lax.broadcasted_iota(jnp.int32, shape, 0)
    column = lax.broadcasted_iota(jnp.int32, shape, 1)
    group = row // 8
    ident = first_id + column // 4
    size = jnp.zeros(shape, jnp.int32)
    for g in range(GROUPS):
        size = size + ((ident >> g) & 1)
    has = (ident >> group) & 1
    others = size - has
    weight = jnp.zeros(shape, f32)
    fact = [1.0]
    for n in range(1, GROUPS + 1):
        fact.append(fact[-1] * n)
    for n in range(GROUPS):
        value = fact[n] * fact[GROUPS - 1 - n] / fact[GROUPS]
        weight = jnp.where(others == n, value, weight)
    weight = jnp.where(has == 1, weight, -weight)
    return jnp.where((row % 4 == column % 4) & (group < GROUPS), weight, 0.0)


def kernel(
    base_ref,
    group_ref,
    pre_ref,
    post_ref,
    fin_gain_ref,
    cos_ref,
    sin_ref,
    wq_hbm,
    wk_hbm,
    wv_hbm,
    wo_hbm,
    key_hbm,
    val_hbm,
    ans_hbm,
    out_ref,
    shap_ref,
    w,
    wo,
    key,
    kt,
    val,
    ans,
    groups,
    rows,
    fin,
    capped,
    sums,
    send1,
    recv1,
    send2,
    recv2,
    init_sem,
    chain_recv,
    chain_send,
    fin_recv,
    fin_send,
    small_sem,
):
    l = lax.axis_index("section")
    c = lax.axis_index("coal")
    y = lax.rem(l, 4)
    x = l // 4

    loads = [
        (wq_hbm, w.at[:, pl.ds(0, 256)]),
        (wk_hbm, w.at[:, pl.ds(256, 128)]),
        (wv_hbm, w.at[:, pl.ds(384, 128)]),
        (wo_hbm, wo),
        (key_hbm, key),
        (val_hbm, val),
        (ans_hbm, ans),
    ]
    loads = [
        pltpu.make_async_copy(a, b, init_sem.at[i]) for i, (a, b) in enumerate(loads)
    ]
    for load in loads:
        load.start()

    barrier = pltpu.get_barrier_semaphore()

    def greet(k, carry):
        pl.semaphore_signal(
            barrier, inc=1, device_id=(lax.rem(l + k, SECTIONS), c), device_id_type=MESH
        )
        pl.semaphore_signal(
            barrier, inc=1, device_id=(l, lax.rem(c + k, COALS)), device_id_type=MESH
        )
        return carry

    lax.fori_loop(1, 16, greet, 0)
    pl.semaphore_wait(barrier, 30)

    for load in loads:
        load.wait()
    kt[...] = key[...].T

    @pl.when(l == 0)
    def _():
        g = group_ref[...].astype(f32)
        groups[...] = jnp.concatenate([g, g], axis=1)

    def chain_copy(b):
        return pltpu.make_async_remote_copy(
            src_ref=rows.at[b],
            dst_ref=rows.at[b],
            send_sem=chain_send,
            recv_sem=chain_recv.at[b],
            device_id=(lax.rem(l + 1, SECTIONS), c),
            device_id_type=MESH,
        )

    def fin_copy(b, child, sem):
        return pltpu.make_async_remote_copy(
            src_ref=fin.at[b],
            dst_ref=fin.at[b],
            send_sem=fin_send.at[sem],
            recv_sem=fin_recv.at[b],
            device_id=(child, c),
            device_id_type=MESH,
        )

    def spread(b):
        @pl.when(y > 0)
        def _():
            fin_copy(b, l - 1, 0).start()

        @pl.when((l == 15) | (l == 11))
        def _():
            fin_copy(b, l - 4, 1).start()

        @pl.when(l == 15)
        def _():
            fin_copy(b, 3, 2).start()

    def work(b):
        @pl.when(l == 0)
        def _():
            ident = c * 64 + 2 * b + lax.broadcasted_iota(jnp.int32, (R, 1), 0) // 4
            b32 = base_ref[...].astype(f32)
            acc = jnp.concatenate([b32, b32], axis=0)
            for g in range(GROUPS):
                acc = acc + ((ident >> g) & 1).astype(f32) * groups[g]
            rows[b] = acc

        @pl.when(l > 0)
        def _():
            chain_copy(b).wait_recv()

        new = block(
            rows[b], w, wo, kt, val, pre_ref[...], post_ref[...], cos_ref[...], sin_ref[...]
        )

        @pl.when(l < LAST)
        def _():
            rows[b] = new
            chain_copy(b).start()

        @pl.when(l == LAST)
        def _():
            inv = lax.rsqrt(jnp.mean(new * new, axis=-1, keepdims=True) + EPS)
            fin[b] = new * inv * fin_gain_ref[...]
            spread(b)

    away = jnp.where(x == 3, 0, jnp.where(x == 1, 2, 1)) + 3 - y
    lag = 2 * (LAST - l) + 2 * away + 2

    def tick(t, carry):
        @pl.when(t < M)
        def _():
            work(t)

        b = t - lag

        @pl.when((l < LAST) & (b >= 0) & (b < M))
        def _():
            fin_copy(b, l, 0).wait_recv()
            spread(b)

        return carry

    lax.fori_loop(0, M + MAX_LAG, tick, 0)

    def whole(ref, sem):
        return pltpu.make_async_remote_copy(
            src_ref=ref,
            dst_ref=ref,
            send_sem=sem,
            recv_sem=sem,
            device_id=(l, c),
            device_id_type=MESH,
        )

    flat = 128

    def read(i, carry):
        part = fin[pl.ds(i * (flat // R), flat // R)].reshape(flat, D)
        logits = fold(
            lax.dot_general(
                split2(part),
                ans[...],
                (((1,), (1,)), ((), ())),
                preferred_element_type=f32,
            )
        )
        capped[pl.ds(i * flat, flat)] = 30.0 * jnp.tanh(logits * (1.0 / 30.0))
        return carry

    lax.fori_loop(0, 256 // flat, read, 0)

    eye = lax.broadcasted_iota(jnp.int32, (128, 128), 0) == lax.broadcasted_iota(
        jnp.int32, (128, 128), 1
    )
    own = []
    for h in range(2):
        part = jnp.sum(
            jnp.exp(capped[pl.ds(128 * h, 128)]), axis=-1, keepdims=True
        )
        own.append(jnp.sum(jnp.where(eye, part, 0.0), axis=0, keepdims=True))
    sums[l] = jnp.concatenate(own + [jnp.zeros((6, 128), f32)], axis=0)

    def sums_copy(peer):
        return pltpu.make_async_remote_copy(
            src_ref=sums.at[l],
            dst_ref=sums.at[l],
            send_sem=small_sem.at[0],
            recv_sem=small_sem.at[1],
            device_id=(peer, c),
            device_id_type=MESH,
        )

    def send_sums(k, carry):
        sums_copy(lax.rem(l + k, SECTIONS)).start()
        return carry

    lax.fori_loop(1, 16, send_sums, 0)
    all_sums = whole(sums.at[pl.ds(0, 15)], small_sem.at[0])
    all_sums.wait_send()
    whole(sums.at[pl.ds(0, 15)], small_sem.at[1]).wait_recv()
    logs = jnp.log(jnp.sum(sums[...], axis=0))
    for h in range(2):
        column = jnp.sum(
            jnp.where(eye, logs[h : h + 1, :], 0.0), axis=1, keepdims=True
        )
        capped[pl.ds(128 * h, 128)] = capped[pl.ds(128 * h, 128)] - column

    values = capped[...]
    shap = jnp.dot(
        shapley_weights(c * 64),
        values,
        preferred_element_type=f32,
        precision=lax.Precision.HIGHEST,
    )
    coeffs = values.reshape(M, R, CANDS)
    upper = lax.broadcasted_iota(jnp.int32, (M, R, CANDS), 1) >= 4
    lower = jnp.concatenate([coeffs[:, 4:], coeffs[:, :4]], axis=1)
    coeffs = coeffs - jnp.where(upper, lower, 0.0)
    for bit in range(5):
        step = 1 << bit
        pairs = coeffs.reshape(M // (2 * step), 2, step, R, CANDS)
        coeffs = jnp.concatenate(
            [pairs[:, :1], pairs[:, 1:] - pairs[:, :1]], axis=1
        ).reshape(M, R, CANDS)
    send1[:, 0:2] = coeffs.reshape(16, 2, R, CANDS)
    send1[:, 2] = shap.reshape(16, 8, CANDS)
    recv1[c] = send1[c]

    def copy1(peer):
        return pltpu.make_async_remote_copy(
            src_ref=send1.at[peer],
            dst_ref=recv1.at[c],
            send_sem=small_sem.at[2],
            recv_sem=small_sem.at[3],
            device_id=(l, peer),
            device_id_type=MESH,
        )

    def start1(k, carry):
        copy1(lax.rem(c + k, COALS)).start()
        return carry

    lax.fori_loop(1, 16, start1, 0)
    whole(send1.at[pl.ds(0, 15)], small_sem.at[2]).wait_send()
    whole(recv1.at[pl.ds(0, 15)], small_sem.at[3]).wait_recv()

    got = recv1[:, 0:2]
    for bit in range(4):
        step = 1 << bit
        pairs = got.reshape(COALS // (2 * step), 2, step, 2, R, CANDS)
        got = jnp.concatenate(
            [pairs[:, :1], pairs[:, 1:] - pairs[:, :1]], axis=1
        ).reshape(COALS, 2, R, CANDS)
    send2[:, 0:2] = got
    total = jnp.sum(recv1[:, 2], axis=0)
    send2[:, 2] = jnp.broadcast_to(total[None], (COALS, R, CANDS))
    recv2[c] = send2[c]

    def copy2(peer):
        return pltpu.make_async_remote_copy(
            src_ref=send2.at[peer],
            dst_ref=recv2.at[c],
            send_sem=small_sem.at[4],
            recv_sem=small_sem.at[5],
            device_id=(l, peer),
            device_id_type=MESH,
        )

    def start2(k, carry):
        copy2(lax.rem(c + k, COALS)).start()
        return carry

    lax.fori_loop(1, 16, start2, 0)
    whole(send2.at[pl.ds(0, 15)], small_sem.at[4]).wait_send()
    whole(recv2.at[pl.ds(0, 15)], small_sem.at[5]).wait_recv()
    out_ref[...] = recv2[:, 0:2].reshape(M, R, CANDS)
    shap_ref[...] = recv2[0:GROUPS, 2]

    @pl.when(l < LAST)
    def _():
        whole(rows, chain_send).wait_send()

    @pl.when(y > 0)
    def _():
        whole(fin, fin_send.at[0]).wait_send()

    @pl.when((l == 15) | (l == 11))
    def _():
        whole(fin, fin_send.at[1]).wait_send()

    @pl.when(l == 15)
    def _():
        whole(fin, fin_send.at[2]).wait_send()


def per_device(
    base_rows,
    group_out,
    pre_gain,
    w_query,
    w_key,
    w_value,
    w_out,
    post_gain,
    key_cache,
    value_cache,
    final_gain,
    answer_rows,
):
    cosine, sine = rope_rows()
    vmem = pl.BlockSpec(memory_space=pltpu.VMEM)
    hbm = pl.BlockSpec(memory_space=pl.ANY)
    exchange = pltpu.VMEM((16, 3, R, CANDS), f32)
    coeffs, shapley = pl.pallas_call(
        kernel,
        out_shape=(
            jax.ShapeDtypeStruct((M, R, CANDS), f32),
            jax.ShapeDtypeStruct((GROUPS, 8, CANDS), f32),
        ),
        in_specs=[vmem] * 7 + [hbm] * 7,
        out_specs=(vmem, vmem),
        scratch_shapes=[
            pltpu.VMEM((D, 512), bf16),
            pltpu.VMEM((256, D), bf16),
            pltpu.VMEM((PREFIX, HEAD), bf16),
            pltpu.VMEM((HEAD, PREFIX), bf16),
            pltpu.VMEM((PREFIX, HEAD), bf16),
            pltpu.VMEM((CANDS, D), bf16),
            pltpu.VMEM((GROUPS, R, D), f32),
            pltpu.VMEM((M, R, D), f32),
            pltpu.VMEM((M, R, D), f32),
            pltpu.VMEM((M * R, CANDS), f32),
            pltpu.VMEM((SECTIONS, 8, 128), f32),
            exchange,
            exchange,
            exchange,
            exchange,
            pltpu.SemaphoreType.DMA((7,)),
            pltpu.SemaphoreType.DMA((M,)),
            pltpu.SemaphoreType.DMA,
            pltpu.SemaphoreType.DMA((M,)),
            pltpu.SemaphoreType.DMA((3,)),
            pltpu.SemaphoreType.DMA((6,)),
        ],
        compiler_params=pltpu.CompilerParams(
            collective_id=0, has_side_effects=True, vmem_limit_bytes=58 << 20
        ),
    )(
        base_rows,
        group_out,
        pre_gain,
        post_gain,
        final_gain.reshape(1, D),
        jnp.asarray(cosine),
        jnp.asarray(sine),
        w_query[0],
        w_key[0],
        w_value[0],
        w_out[0],
        key_cache[0],
        value_cache[0],
        answer_rows,
    )
    return coeffs.reshape(64, 4, CANDS), shapley[:, :4]


def solution(mesh):
    placed = (
        P(),
        P(),
        P("section", None),
        P("section", None, None),
        P("section", None, None),
        P("section", None, None),
        P("section", None, None),
        P("section", None),
        P("section", None, None),
        P("section", None, None),
        P(),
        P("section", None),
    )
    return jax.shard_map(
        per_device,
        mesh=mesh,
        in_specs=placed,
        out_specs=(P("coal", None, "section"), P(None, None, "section")),
        check_vma=False,
    )
```

```python
import functools

import jax
import jax.numpy as jnp
import numpy as np
from jax import lax
from jax.experimental import pallas as pl
from jax.experimental.pallas import tpu as pltpu
from jax.sharding import PartitionSpec as P

f32, bf16 = jnp.float32, jnp.bfloat16
MESH = pl.DeviceIdType.MESH

D = 4608
HEAD = 128
PREFIX = 2048
GROUPS = 10
SECTIONS = 16
COALS = 16
R = 8
M = 32
CANDS = 256
EPS = 1e-6
LAST = SECTIONS - 1
CHUNKS = 4
DEPTH = 3
WIDE = D // CHUNKS
GROUP = 8
N_GROUPS = M // GROUP
G_ROWS = GROUP * R
HOP = 60
MAX_LAG = 40
LATE = 26


def rope_rows():
    half = HEAD // 2
    places = PREFIX + np.arange(R) % 4
    inverse = 10000.0 ** (-2.0 * np.arange(half) / HEAD)
    angles = places[:, None] * inverse[None, :]
    cosine, sine = np.cos(angles), np.sin(angles)
    return (
        np.concatenate([cosine, cosine], axis=1).astype(np.float32),
        np.concatenate([-sine, sine], axis=1).astype(np.float32),
    )


def split2(x):
    high = x.astype(bf16).astype(f32)
    return jnp.concatenate([high, x - high], axis=0).astype(bf16)


def fold(y):
    half = y.shape[0] // 2
    return y[:half] + y[half:]


def dot(left, right):
    return jnp.dot(left, right, preferred_element_type=f32)


def attention(y, kt_ref, v_ref, cosine, sine):
    rows = y.shape[0]

    def rotated(z):
        return z * cosine + pltpu.roll(z, HEAD // 2, 1) * sine

    q = jnp.concatenate([rotated(y[:, :128]), rotated(y[:, 128:256])], axis=0)
    q = q * (1.0 / 600.0)
    k = rotated(y[:, 256:384])
    v = y[:, 384:512]
    p = jnp.exp(50.0 * jnp.tanh(fold(dot(split2(q), kt_ref[...]))))
    mixed = fold(dot(split2(p), v_ref[...]))
    total = jnp.sum(p, axis=-1, keepdims=True)
    place = lax.broadcasted_iota(jnp.int32, (2 * rows, 1), 0) % 4
    for back in range(4):
        k_back = pltpu.roll(k, back, 0) if back else k
        v_back = pltpu.roll(v, back, 0) if back else v
        score = jnp.sum(
            q * jnp.concatenate([k_back, k_back], axis=0), axis=-1, keepdims=True
        )
        weight = jnp.where(place >= back, jnp.exp(50.0 * jnp.tanh(score)), 0.0)
        total = total + weight
        mixed = mixed + weight * jnp.concatenate([v_back, v_back], axis=0)
    attended = mixed / total
    return jnp.concatenate([attended[:rows], attended[rows:]], axis=1)


def shapley_weights(first_id):
    shape = (16 * 8, G_ROWS)
    row = lax.broadcasted_iota(jnp.int32, shape, 0)
    column = lax.broadcasted_iota(jnp.int32, shape, 1)
    group = row // 8
    ident = first_id + column // 4
    size = jnp.zeros(shape, jnp.int32)
    for g in range(GROUPS):
        size = size + ((ident >> g) & 1)
    has = (ident >> group) & 1
    others = size - has
    weight = jnp.zeros(shape, f32)
    fact = [1.0]
    for n in range(1, GROUPS + 1):
        fact.append(fact[-1] * n)
    for n in range(GROUPS):
        value = fact[n] * fact[GROUPS - 1 - n] / fact[GROUPS]
        weight = jnp.where(others == n, value, weight)
    weight = jnp.where(has == 1, weight, -weight)
    return jnp.where((row % 4 == column % 4) & (group < GROUPS), weight, 0.0)


def kernel(
    base_ref,
    group_ref,
    pre_ref,
    post_ref,
    fin_gain_ref,
    cos_ref,
    sin_ref,
    wq_hbm,
    wk_hbm,
    wv_hbm,
    wo_hbm,
    key_hbm,
    val_hbm,
    ans_hbm,
    out_ref,
    shap_ref,
    w,
    wo,
    key,
    kt,
    val,
    ans,
    ans_t,
    groups,
    rows,
    fin,
    capped,
    sums,
    send1,
    recv1,
    send2,
    recv2,
    init_sem,
    chain_recv,
    chain_send,
    fin_recv,
    fin_send,
    tail_send,
    tail_recv,
):
    l = lax.axis_index("section")
    c = lax.axis_index("coal")
    y = lax.rem(l, 4)
    x = l // 4

    loads = [
        (wq_hbm, w.at[:, pl.ds(0, 256)]),
        (wk_hbm, w.at[:, pl.ds(256, 128)]),
        (wv_hbm, w.at[:, pl.ds(384, 128)]),
        (key_hbm, key),
        (val_hbm, val),
        (wo_hbm, wo),
        (ans_hbm, ans),
    ]
    loads = [
        pltpu.make_async_copy(a, b, init_sem.at[i]) for i, (a, b) in enumerate(loads)
    ]
    for load in loads:
        load.start()

    barrier = pltpu.get_barrier_semaphore()

    def greet(k, carry):
        pl.semaphore_signal(
            barrier, inc=1, device_id=(lax.rem(l + k, SECTIONS), c), device_id_type=MESH
        )
        pl.semaphore_signal(
            barrier, inc=1, device_id=(l, lax.rem(c + k, COALS)), device_id_type=MESH
        )
        return carry

    lax.fori_loop(1, 16, greet, 0)

    @pl.when(l == 0)
    def _():
        g = group_ref[...].astype(f32)
        groups[...] = jnp.concatenate([g, g], axis=1)

    for load in loads:
        load.wait()
    kt[...] = key[...].T

    def turn_answers():
        def turn(i, carry):
            at = pl.multiple_of(i * 128, 128)
            ans_t[pl.ds(at, 128), :] = ans[:, pl.ds(at, 128)].T
            return carry

        lax.fori_loop(0, D // 128, turn, 0)

    @pl.when(l > 0)
    def _():
        turn_answers()

    pl.semaphore_wait(barrier, 30)

    def part(j):
        return pl.ds(j * WIDE, WIDE)

    def chain_copy(b, j):
        return pltpu.make_async_remote_copy(
            src_ref=rows.at[b, :, part(j)],
            dst_ref=rows.at[b, :, part(j)],
            send_sem=chain_send.at[lax.rem(b, DEPTH)],
            recv_sem=chain_recv.at[b, j],
            device_id=(lax.rem(l + 1, SECTIONS), c),
            device_id_type=MESH,
        )

    def fin_copy(b, child, sem):
        return pltpu.make_async_remote_copy(
            src_ref=fin.at[b],
            dst_ref=fin.at[b],
            send_sem=fin_send.at[sem],
            recv_sem=fin_recv.at[b],
            device_id=(child, c),
            device_id_type=MESH,
        )

    def spread(b):
        @pl.when((l == 15) | (l == 11))
        def _():
            fin_copy(b, l - 4, 1).start()

        @pl.when(l == 15)
        def _():
            fin_copy(b, 3, 2).start()

        @pl.when((y > 1) | ((y == 1) & (b < LATE)))
        def _():
            fin_copy(b, l - 1, 0).start()

        @pl.when((y == 3) & (b >= LATE))
        def _():
            fin_copy(b, l - 3, 3).start()

    def whole(ref, sem):
        return pltpu.make_async_remote_copy(
            src_ref=ref,
            dst_ref=ref,
            send_sem=sem,
            recv_sem=sem,
            device_id=(l, c),
            device_id_type=MESH,
        )

    def work(b):
        @pl.when(l == 0)
        def _():
            ident = c * 64 + 2 * b + lax.broadcasted_iota(jnp.int32, (R, 1), 0) // 4
            b32 = base_ref[...].astype(f32)
            acc = jnp.concatenate([b32, b32], axis=0)
            for g in range(GROUPS):
                acc = acc + ((ident >> g) & 1).astype(f32) * groups[g]
            rows[b] = acc

        square = jnp.zeros((R, 1), f32)
        mixed = jnp.zeros((2 * R, 512), f32)
        for j in range(CHUNKS):

            @pl.when(l > 0)
            def _():
                chain_copy(b, j).wait_recv()

            piece = rows[b, :, part(j)]
            square = square + jnp.sum(piece * piece, axis=-1, keepdims=True)
            mixed = mixed + dot(split2(piece * pre_ref[:, part(j)]), w[part(j), :])
        inv = lax.rsqrt(square * (1.0 / D) + EPS)
        attended = attention(fold(mixed) * inv, kt, val, cos_ref[...], sin_ref[...])
        proj = fold(dot(split2(attended), wo[...]))
        scale = lax.rsqrt(jnp.mean(proj * proj, axis=-1, keepdims=True) + EPS)

        @pl.when((l < LAST) & (b >= DEPTH))
        def _():
            whole(rows.at[b - DEPTH], chain_send.at[lax.rem(b, DEPTH)]).wait_send()

        @pl.when(l < LAST)
        def _():
            for j in range(CHUNKS):
                rows[b, :, part(j)] = (
                    rows[b, :, part(j)]
                    + proj[:, j * WIDE : (j + 1) * WIDE] * scale * post_ref[:, part(j)]
                )
                chain_copy(b, j).start()

        @pl.when(l == LAST)
        def _():
            new = rows[b] + proj * scale * post_ref[...]
            inv = lax.rsqrt(jnp.mean(new * new, axis=-1, keepdims=True) + EPS)
            fin[b] = new * inv * fin_gain_ref[...]
            spread(b)

    eye = lax.broadcasted_iota(jnp.int32, (G_ROWS, 128), 0) == lax.broadcasted_iota(
        jnp.int32, (G_ROWS, 128), 1
    )

    def read(g):
        block = fin[pl.ds(g * GROUP, GROUP)].reshape(G_ROWS, D)
        logits = fold(dot(split2(block), ans_t[...]))
        values = 30.0 * jnp.tanh(logits * (1.0 / 30.0))
        capped[g] = values
        column = jnp.sum(jnp.exp(values), axis=-1, keepdims=True)
        line = jnp.sum(jnp.where(eye, column, 0.0), axis=0, keepdims=True)
        mine = g * SECTIONS + l
        sums[mine] = jnp.broadcast_to(line, (8, 128))

        def send(k, carry):
            pltpu.make_async_remote_copy(
                src_ref=sums.at[mine],
                dst_ref=sums.at[mine],
                send_sem=tail_send.at[0],
                recv_sem=tail_recv.at[0, g],
                device_id=(lax.rem(l + k, SECTIONS), c),
                device_id_type=MESH,
            ).start()
            return carry

        lax.fori_loop(1, 16, send, 0)

    def exchange(src, dst, g, kind):
        def send(k, carry):
            peer = lax.rem(c + k, COALS)
            pltpu.make_async_remote_copy(
                src_ref=src.at[g * COALS + peer],
                dst_ref=dst.at[g * COALS + c],
                send_sem=tail_send.at[kind],
                recv_sem=tail_recv.at[kind, g],
                device_id=(l, peer),
                device_id_type=MESH,
            ).start()
            return carry

        lax.fori_loop(1, 16, send, 0)
        dst[g * COALS + c] = src[g * COALS + c]

    def scatter(g):
        whole(sums.at[pl.ds(0, 15)], tail_recv.at[0, g]).wait_recv()
        logs = jnp.log(jnp.sum(sums[pl.ds(g * SECTIONS, SECTIONS)], axis=0)[0:1])
        column = jnp.sum(jnp.where(eye, logs, 0.0), axis=1, keepdims=True)
        values = capped[g] - column
        shap = jnp.dot(
            shapley_weights(c * 64 + g * (2 * GROUP)),
            values,
            preferred_element_type=f32,
            precision=lax.Precision.HIGHEST,
        ).reshape(16, 8, CANDS)
        low = lax.broadcasted_iota(jnp.int32, (16, 8, 128), 1) < 4
        shap = jnp.where(low, shap[:, :, :128], shap[:, :, 128:])
        values = values.reshape(GROUP, R, CANDS)
        for i in range(GROUP):
            for h in range(2):
                send1[g * COALS + 2 * i + h, 0] = values[i, :, 128 * h : 128 * h + 128]
        send1[pl.ds(g * COALS, COALS), 1] = shap
        exchange(send1, recv1, g, 1)

    def gather(g):
        whole(recv1.at[pl.ds(0, 15)], tail_recv.at[1, g]).wait_recv()
        slots = pl.ds(g * COALS, COALS)
        got = recv1[slots, 0]
        for bit in range(4):
            step = 1 << bit
            pairs = got.reshape(COALS // (2 * step), 2, step, 8, 128)
            got = jnp.concatenate(
                [pairs[:, :1], pairs[:, 1:] - pairs[:, :1]], axis=1
            ).reshape(COALS, 8, 128)
        total = jnp.sum(recv1[slots, 1], axis=0)
        send2[slots, 0] = got
        send2[slots, 1] = jnp.broadcast_to(total[None], (COALS, 8, 128))
        exchange(send2, recv2, g, 2)

    away = jnp.where(x == 3, 0, jnp.where(x == 1, 2, 1)) + 3 - y
    lag = (HOP * (LAST - l) + 10 + 45 * away + 32) // 33
    lag = jnp.where(l == LAST, 0, jnp.where(l == 0, MAX_LAG, lag))

    def tick(t, carry):
        @pl.when(t < M)
        def _():
            work(t)

        @pl.when((l == 0) & (t == M))
        def _():
            turn_answers()

        b = t - lag

        @pl.when((l < LAST) & (b >= 0) & (b < M))
        def _():
            fin_copy(b, l, 0).wait_recv()
            spread(b)

        @pl.when((b >= 0) & (b < M) & (lax.rem(b, GROUP) == GROUP - 1))
        def _():
            read(b // GROUP)

        @pl.when((b >= 18) & (lax.rem(b, GROUP) == 2) & (b <= M + 10))
        def _():
            scatter(b // GROUP - 2)

        @pl.when((b >= 20) & (lax.rem(b, GROUP) == 4) & (b <= M + 12))
        def _():
            gather(b // GROUP - 2)

        return carry

    lax.fori_loop(0, M + MAX_LAG + 13, tick, 0)

    for g in range(N_GROUPS):
        whole(recv2.at[pl.ds(0, 15)], tail_recv.at[2, g]).wait_recv()
    coeffs = recv2[:, 0].reshape(M, 2, 8, 128)
    coeffs = jnp.concatenate([coeffs[:, 0], coeffs[:, 1]], axis=-1)
    upper = lax.broadcasted_iota(jnp.int32, (M, R, CANDS), 1) >= 4
    lower = jnp.concatenate([coeffs[:, 4:], coeffs[:, :4]], axis=1)
    coeffs = coeffs - jnp.where(upper, lower, 0.0)
    for bit in range(5):
        step = 1 << bit
        pairs = coeffs.reshape(M // (2 * step), 2, step, R, CANDS)
        coeffs = jnp.concatenate(
            [pairs[:, :1], pairs[:, 1:] - pairs[:, :1]], axis=1
        ).reshape(M, R, CANDS)
    out_ref[...] = coeffs
    shap_ref[...] = jnp.sum(
        recv2[:, 1].reshape(N_GROUPS, COALS, 8, 128), axis=0
    )[:GROUPS]

    for kind, ref in enumerate([sums, send1, send2]):
        whole(ref.at[pl.ds(0, 15 * N_GROUPS)], tail_send.at[kind]).wait_send()

    @pl.when(l < LAST)
    def _():
        for b in range(M - DEPTH, M):
            whole(rows.at[b], chain_send.at[b % DEPTH]).wait_send()

    @pl.when(y > 1)
    def _():
        whole(fin, fin_send.at[0]).wait_send()

    @pl.when(y == 1)
    def _():
        whole(fin.at[pl.ds(0, LATE)], fin_send.at[0]).wait_send()

    @pl.when(y == 3)
    def _():
        whole(fin.at[pl.ds(LATE, M - LATE)], fin_send.at[3]).wait_send()

    @pl.when((l == 15) | (l == 11))
    def _():
        whole(fin, fin_send.at[1]).wait_send()

    @pl.when(l == 15)
    def _():
        whole(fin, fin_send.at[2]).wait_send()


def per_device(
    base_rows,
    group_out,
    pre_gain,
    w_query,
    w_key,
    w_value,
    w_out,
    post_gain,
    key_cache,
    value_cache,
    final_gain,
    answer_rows,
):
    cosine, sine = rope_rows()
    vmem = pl.BlockSpec(memory_space=pltpu.VMEM)
    hbm = pl.BlockSpec(memory_space=pl.ANY)
    exchange = pltpu.VMEM((N_GROUPS * COALS, 2, 8, 128), f32)
    coeffs, shapley = pl.pallas_call(
        kernel,
        out_shape=(
            jax.ShapeDtypeStruct((M, R, CANDS), f32),
            jax.ShapeDtypeStruct((GROUPS, 8, 128), f32),
        ),
        in_specs=[vmem] * 7 + [hbm] * 7,
        out_specs=(vmem, vmem),
        scratch_shapes=[
            pltpu.VMEM((D, 512), bf16),
            pltpu.VMEM((256, D), bf16),
            pltpu.VMEM((PREFIX, HEAD), bf16),
            pltpu.VMEM((HEAD, PREFIX), bf16),
            pltpu.VMEM((PREFIX, HEAD), bf16),
            pltpu.VMEM((CANDS, D), bf16),
            pltpu.VMEM((D, CANDS), bf16),
            pltpu.VMEM((GROUPS, R, D), f32),
            pltpu.VMEM((M, R, D), f32),
            pltpu.VMEM((M, R, D), f32),
            pltpu.VMEM((N_GROUPS, G_ROWS, CANDS), f32),
            pltpu.VMEM((N_GROUPS * SECTIONS, 8, 128), f32),
            exchange,
            exchange,
            exchange,
            exchange,
            pltpu.SemaphoreType.DMA((7,)),
            pltpu.SemaphoreType.DMA((M, CHUNKS)),
            pltpu.SemaphoreType.DMA((DEPTH,)),
            pltpu.SemaphoreType.DMA((M,)),
            pltpu.SemaphoreType.DMA((4,)),
            pltpu.SemaphoreType.DMA((3,)),
            pltpu.SemaphoreType.DMA((3, N_GROUPS)),
        ],
        compiler_params=pltpu.CompilerParams(
            collective_id=0, has_side_effects=True, vmem_limit_bytes=58 << 20
        ),
    )(
        base_rows,
        group_out,
        pre_gain,
        post_gain,
        final_gain.reshape(1, D),
        jnp.asarray(cosine),
        jnp.asarray(sine),
        w_query[0],
        w_key[0],
        w_value[0],
        w_out[0],
        key_cache[0],
        value_cache[0],
        answer_rows,
    )
    shapley = shapley.reshape(GROUPS, 2, 4, 128).transpose(0, 2, 1, 3)
    return coeffs.reshape(64, 4, CANDS), shapley.reshape(GROUPS, 4, CANDS)


def solution(mesh):
    placed = (
        P(),
        P(),
        P("section", None),
        P("section", None, None),
        P("section", None, None),
        P("section", None, None),
        P("section", None, None),
        P("section", None),
        P("section", None, None),
        P("section", None, None),
        P(),
        P("section", None),
    )
    return jax.shard_map(
        per_device,
        mesh=mesh,
        in_specs=placed,
        out_specs=(P("coal", None, "section"), P(None, None, "section")),
        check_vma=False,
    )
```

```python
import functools

import jax
import jax.numpy as jnp
import numpy as np
from jax import lax
from jax.experimental import pallas as pl
from jax.experimental.pallas import tpu as pltpu
from jax.sharding import PartitionSpec as P

f32, bf16 = jnp.float32, jnp.bfloat16
MESH = pl.DeviceIdType.MESH

D = 4608
HEAD = 128
PREFIX = 2048
GROUPS = 10
SECTIONS = 16
COALS = 16
R = 8
M = 32
CANDS = 256
EPS = 1e-6
LAST = SECTIONS - 1
CHUNKS = 4
DEPTH = 3
WIDE = D // CHUNKS
GROUP = 16
HALF = GROUP // 2
N_GROUPS = M // GROUP
G_ROWS = GROUP * R
END = 2
E_ROWS = END * R
HOP = 60
MAX_LAG = 40
FAR_FIRST = (8, 7, 9, 6, 10, 5, 11, 4, 12, 3, 13, 2, 14, 1, 15)
FIN_CHUNKS = 4
FIN_WIDE = D // FIN_CHUNKS
LATE = 26


def rope_rows():
    half = HEAD // 2
    places = PREFIX + np.arange(R) % 4
    inverse = 10000.0 ** (-2.0 * np.arange(half) / HEAD)
    angles = places[:, None] * inverse[None, :]
    cosine, sine = np.cos(angles), np.sin(angles)
    return (
        np.concatenate([cosine, cosine], axis=1).astype(np.float32),
        np.concatenate([-sine, sine], axis=1).astype(np.float32),
    )


def split2(x):
    high = x.astype(bf16).astype(f32)
    return jnp.concatenate([high, x - high], axis=0).astype(bf16)


def fold(y):
    half = y.shape[0] // 2
    return y[:half] + y[half:]


def dot(left, right):
    return jnp.dot(left, right, preferred_element_type=f32)


def attention(y, kt_ref, v_ref, cosine, sine):
    rows = y.shape[0]

    def rotated(z):
        return z * cosine + pltpu.roll(z, HEAD // 2, 1) * sine

    q = jnp.concatenate([rotated(y[:, :128]), rotated(y[:, 128:256])], axis=0)
    q = q * (1.0 / 600.0)
    k = rotated(y[:, 256:384])
    v = y[:, 384:512]
    p = jnp.exp(50.0 * jnp.tanh(fold(dot(split2(q), kt_ref[...]))))
    mixed = fold(dot(split2(p), v_ref[...]))
    total = jnp.sum(p, axis=-1, keepdims=True)
    place = lax.broadcasted_iota(jnp.int32, (2 * rows, 1), 0) % 4
    for back in range(4):
        k_back = pltpu.roll(k, back, 0) if back else k
        v_back = pltpu.roll(v, back, 0) if back else v
        score = jnp.sum(
            q * jnp.concatenate([k_back, k_back], axis=0), axis=-1, keepdims=True
        )
        weight = jnp.where(place >= back, jnp.exp(50.0 * jnp.tanh(score)), 0.0)
        total = total + weight
        mixed = mixed + weight * jnp.concatenate([v_back, v_back], axis=0)
    attended = mixed / total
    return jnp.concatenate([attended[:rows], attended[rows:]], axis=1)


def shapley_weights(shape, ident_of):
    row = lax.broadcasted_iota(jnp.int32, shape, 0)
    column = lax.broadcasted_iota(jnp.int32, shape, 1)
    group = row // 8
    ident = ident_of(column)
    size = jnp.zeros(shape, jnp.int32)
    for g in range(GROUPS):
        size = size + ((ident >> g) & 1)
    has = (ident >> group) & 1
    others = size - has
    weight = jnp.zeros(shape, f32)
    fact = [1.0]
    for n in range(1, GROUPS + 1):
        fact.append(fact[-1] * n)
    for n in range(GROUPS):
        value = fact[n] * fact[GROUPS - 1 - n] / fact[GROUPS]
        weight = jnp.where(others == n, value, weight)
    weight = jnp.where(has == 1, weight, -weight)
    return jnp.where((row % 4 == column % 4) & (group < GROUPS), weight, 0.0)


def kernel(
    base_ref,
    group_ref,
    pre_ref,
    post_ref,
    fin_gain_ref,
    cos_ref,
    sin_ref,
    wq_hbm,
    wk_hbm,
    wv_hbm,
    wo_hbm,
    key_hbm,
    val_hbm,
    ans_hbm,
    out_ref,
    shap_ref,
    w,
    wo,
    key,
    kt,
    val,
    ans,
    ans_t,
    groups,
    rows,
    fin,
    capped,
    sums,
    send1,
    recv1,
    send2,
    recv2,
    ends,
    lines,
    init_sem,
    chain_recv,
    chain_send,
    fin_recv,
    fin_send,
    tail_send,
    tail_recv,
):
    l = lax.axis_index("section")
    c = lax.axis_index("coal")
    y = lax.rem(l, 4)
    x = l // 4

    loads = [
        (wq_hbm, w.at[:, pl.ds(0, 256)]),
        (wk_hbm, w.at[:, pl.ds(256, 128)]),
        (wv_hbm, w.at[:, pl.ds(384, 128)]),
        (key_hbm, key),
        (val_hbm, val),
        (wo_hbm, wo),
        (ans_hbm, ans),
    ]
    loads = [
        pltpu.make_async_copy(a, b, init_sem.at[i]) for i, (a, b) in enumerate(loads)
    ]
    for load in loads:
        load.start()

    barrier = pltpu.get_barrier_semaphore()

    def greet(device):
        pl.semaphore_signal(barrier, inc=1, device_id=device, device_id_type=MESH)

    def greet_coal():
        for k in range(1, COALS):
            greet((l, lax.rem(c + k, COALS)))

    @pl.when(l == 0)
    def _():
        greet_coal()

    for k in range(SECTIONS):

        @pl.when(l != k)
        def _():
            greet((k, c))

    @pl.when(l != 0)
    def _():
        greet_coal()

    @pl.when(l == 0)
    def _():
        g = group_ref[...].astype(f32)
        groups[...] = jnp.concatenate([g, g], axis=1)

    for load in loads[:-1]:
        load.wait()
    kt[...] = key[...].T

    def turn_answers():
        loads[-1].wait()

        def turn(i, carry):
            at = pl.multiple_of(i * 128, 128)
            ans_t[pl.ds(at, 128), :] = ans[:, pl.ds(at, 128)].T
            return carry

        lax.fori_loop(0, D // 128, turn, 0)

    @pl.when(l > 0)
    def _():
        turn_answers()

    pl.semaphore_wait(barrier, 30)

    def part(j):
        return pl.ds(j * WIDE, WIDE)

    def chain_copy(b, j):
        return pltpu.make_async_remote_copy(
            src_ref=rows.at[b, :, part(j)],
            dst_ref=rows.at[b, :, part(j)],
            send_sem=chain_send.at[lax.rem(b, DEPTH)],
            recv_sem=chain_recv.at[b, j],
            device_id=(lax.rem(l + 1, SECTIONS), c),
            device_id_type=MESH,
        )

    def fin_copy(b, f, child, sem):
        piece = fin.at[b, :, pl.ds(f * FIN_WIDE, FIN_WIDE)]
        return pltpu.make_async_remote_copy(
            src_ref=piece,
            dst_ref=piece,
            send_sem=fin_send.at[sem],
            recv_sem=fin_recv.at[b, f],
            device_id=(child, c),
            device_id_type=MESH,
        )

    def spread(b, f):
        @pl.when((l == 15) | (l == 11))
        def _():
            fin_copy(b, f, l - 4, 1).start()

        @pl.when(l == 15)
        def _():
            fin_copy(b, f, 3, 2).start()

        @pl.when((y > 1) | ((y == 1) & (b < LATE)))
        def _():
            fin_copy(b, f, l - 1, 0).start()

        @pl.when((y == 3) & (b >= LATE))
        def _():
            fin_copy(b, f, l - 3, 3).start()

    def whole(ref, sem):
        return pltpu.make_async_remote_copy(
            src_ref=ref,
            dst_ref=ref,
            send_sem=sem,
            recv_sem=sem,
            device_id=(l, c),
            device_id_type=MESH,
        )

    def work(b):
        @pl.when(l == 0)
        def _():
            ident = c * 64 + 2 * b + lax.broadcasted_iota(jnp.int32, (R, 1), 0) // 4
            b32 = base_ref[...].astype(f32)
            acc = jnp.concatenate([b32, b32], axis=0)
            for g in range(GROUPS):
                acc = acc + ((ident >> g) & 1).astype(f32) * groups[g]
            rows[b] = acc

        square = jnp.zeros((R, 1), f32)
        mixed = jnp.zeros((2 * R, 512), f32)
        for j in range(CHUNKS):

            @pl.when(l > 0)
            def _():
                chain_copy(b, j).wait_recv()

            piece = rows[b, :, part(j)]
            square = square + jnp.sum(piece * piece, axis=-1, keepdims=True)
            mixed = mixed + dot(split2(piece * pre_ref[:, part(j)]), w[part(j), :])
        inv = lax.rsqrt(square * (1.0 / D) + EPS)
        attended = attention(fold(mixed) * inv, kt, val, cos_ref[...], sin_ref[...])
        proj = fold(dot(split2(attended), wo[...]))
        scale = lax.rsqrt(jnp.mean(proj * proj, axis=-1, keepdims=True) + EPS)

        @pl.when((l < LAST) & (b >= DEPTH))
        def _():
            whole(rows.at[b - DEPTH], chain_send.at[lax.rem(b, DEPTH)]).wait_send()

        @pl.when(l < LAST)
        def _():
            for j in range(CHUNKS):
                rows[b, :, part(j)] = (
                    rows[b, :, part(j)]
                    + proj[:, j * WIDE : (j + 1) * WIDE] * scale * post_ref[:, part(j)]
                )
                chain_copy(b, j).start()

        @pl.when(l == LAST)
        def _():
            new = rows[b] + proj * scale * post_ref[...]
            inv = lax.rsqrt(jnp.mean(new * new, axis=-1, keepdims=True) + EPS)
            fin[b] = new * inv * fin_gain_ref[...].reshape(1, D)
            for f in range(FIN_CHUNKS):
                spread(b, f)

    def eye(shape):
        return lax.broadcasted_iota(jnp.int32, shape, len(shape) - 2) == (
            lax.broadcasted_iota(jnp.int32, shape, len(shape) - 1)
        )

    def score(first, count):
        block = fin[pl.ds(first, count)].reshape(count * R, D)
        logits = fold(dot(split2(block), ans_t[...]))
        return 30.0 * jnp.tanh(logits * (1.0 / 30.0))

    def line_of(values, lane):
        n = values.shape[0]
        column = jnp.sum(jnp.exp(values), axis=-1, keepdims=True)
        here = lax.broadcasted_iota(jnp.int32, (n, 128), 0) + lane
        here = here == lax.broadcasted_iota(jnp.int32, (n, 128), 1)
        line = jnp.sum(jnp.where(here, column, 0.0), axis=0, keepdims=True)
        return jnp.broadcast_to(line, (8, 128))

    def read(first, count, g, lane):
        values = score(first, count)
        capped[g, pl.ds(lane, count * R)] = values
        mine = g * SECTIONS + l
        line = line_of(values, lane)
        sums[mine] = line if lane == 0 else sums[mine] + line

    def send_sums(slot):
        mine = slot * SECTIONS + l
        for k in FAR_FIRST:
            pltpu.make_async_remote_copy(
                src_ref=sums.at[mine],
                dst_ref=sums.at[mine],
                send_sem=tail_send.at[0],
                recv_sem=tail_recv.at[0, slot],
                device_id=(lax.rem(l + k, SECTIONS), c),
                device_id_type=MESH,
            ).start()

    def read_end():
        values = score(M - END, END)
        ends[c] = values
        sums[N_GROUPS * SECTIONS + l] = line_of(values, 0)
        send_sums(N_GROUPS)
        for k in FAR_FIRST:
            end_copy(lax.rem(c + k, COALS)).start()

    def end_copy(peer):
        return pltpu.make_async_remote_copy(
            src_ref=ends.at[c],
            dst_ref=ends.at[c],
            send_sem=tail_send.at[3],
            recv_sem=tail_recv.at[1, N_GROUPS],
            device_id=(l, peer),
            device_id_type=MESH,
        )

    def logs_of(slot):
        whole(sums.at[pl.ds(0, 15)], tail_recv.at[0, slot]).wait_recv()
        return jnp.log(jnp.sum(sums[pl.ds(slot * SECTIONS, SECTIONS)], axis=0))

    def end_logs():
        lines[c] = logs_of(N_GROUPS)
        for k in FAR_FIRST:
            pltpu.make_async_remote_copy(
                src_ref=lines.at[c],
                dst_ref=lines.at[c],
                send_sem=tail_send.at[4],
                recv_sem=tail_recv.at[2, N_GROUPS],
                device_id=(l, lax.rem(c + k, COALS)),
                device_id_type=MESH,
            ).start()

    def end_result():
        def ident(column):
            return column // E_ROWS * 64 + (64 - 2 * END) + lax.rem(column, E_ROWS) // 4

        weights = shapley_weights((16 * 8, COALS * E_ROWS), ident)
        signs = []
        for other in range(COALS):
            sign = 1
            for bit in range(4):
                has = (c >> bit) & 1
                sign = sign * (has if (other >> bit) & 1 else 1 - 2 * has)
            signs.append(sign.astype(f32))
        whole(ends.at[pl.ds(0, 15)], tail_recv.at[1, N_GROUPS]).wait_recv()
        whole(lines.at[pl.ds(0, 15)], tail_recv.at[2, N_GROUPS]).wait_recv()
        logs = jnp.sum(
            jnp.where(eye((COALS, E_ROWS, 128)), lines[:, 0:1, :], 0.0),
            axis=-1,
            keepdims=True,
        )
        values = ends[...] - logs
        coeffs = signs[0] * values[0]
        for other in range(1, COALS):
            coeffs = coeffs + signs[other] * values[other]
        shap = jnp.dot(
            weights,
            values.reshape(COALS * E_ROWS, CANDS),
            preferred_element_type=f32,
            precision=lax.Precision.HIGHEST,
        )
        return coeffs.reshape(END, R, CANDS), halves(shap)

    def halves(shap):
        shap = shap.reshape(16, 8, CANDS)
        low = lax.broadcasted_iota(jnp.int32, (16, 8, 128), 1) < 4
        return jnp.where(low, shap[:, :, :128], shap[:, :, 128:])

    def exchange(src, dst, g, kind):
        for k in FAR_FIRST:
            peer = lax.rem(c + k, COALS)
            pltpu.make_async_remote_copy(
                src_ref=src.at[g * COALS + peer],
                dst_ref=dst.at[g * COALS + c],
                send_sem=tail_send.at[kind],
                recv_sem=tail_recv.at[kind, g],
                device_id=(l, peer),
                device_id_type=MESH,
            ).start()
        dst[g * COALS + c] = src[g * COALS + c]

    def scatter(g, count):
        n = count * R
        column = jnp.sum(
            jnp.where(eye((n, 128)), logs_of(g)[0:1], 0.0), axis=1, keepdims=True
        )
        values = capped[g, pl.ds(0, n)] - column
        first = c * 64 + g * (2 * GROUP)
        shap = jnp.dot(
            shapley_weights((16 * 8, n), lambda column: first + column // 4),
            values,
            preferred_element_type=f32,
            precision=lax.Precision.HIGHEST,
        )
        values = values.reshape(count, R, CANDS)
        for h in range(2):
            send1[pl.ds(g * COALS, count), h] = values[:, :, 128 * h : 128 * h + 128]
            if count < GROUP:
                send1[pl.ds(g * COALS + count, GROUP - count), h] = jnp.zeros(
                    (GROUP - count, 8, 128), f32
                )
        send1[pl.ds(g * COALS, COALS), 2] = halves(shap)

    def gather(g):
        whole(recv1.at[pl.ds(0, 15)], tail_recv.at[1, g]).wait_recv()
        slots = pl.ds(g * COALS, COALS)
        got = recv1[slots, 0:2]
        for bit in range(4):
            step = 1 << bit
            pairs = got.reshape(COALS // (2 * step), 2, step, 2, 8, 128)
            got = jnp.concatenate(
                [pairs[:, :1], pairs[:, 1:] - pairs[:, :1]], axis=1
            ).reshape(COALS, 2, 8, 128)
        total = jnp.sum(recv1[slots, 2], axis=0)
        send2[slots, 0:2] = got
        send2[slots, 2] = jnp.broadcast_to(total[None], (COALS, 8, 128))

    away = jnp.where(x == 3, 0, jnp.where(x == 1, 2, 1)) + 3 - y
    lag = (HOP * (LAST - l) + 10 + 45 * away + 32) // 33
    lag = jnp.where(l == LAST, 0, jnp.where(l == 0, MAX_LAG, lag))

    def tick(t, carry):
        @pl.when(t < M)
        def _():
            work(t)

        @pl.when((l == 0) & (t == M))
        def _():
            turn_answers()

        b = t - lag

        @pl.when((l < LAST) & (b >= 0) & (b < M))
        def _():
            for f in range(FIN_CHUNKS):
                fin_copy(b, f, l, 0).wait_recv()
                spread(b, f)

        @pl.when(b == HALF - 1)
        def _():
            read(0, HALF, 0, 0)

        @pl.when(b == GROUP - 1)
        def _():
            read(HALF, HALF, 0, HALF * R)

        @pl.when(b == GROUP)
        def _():
            send_sums(0)

        @pl.when(b == GROUP + 6)
        def _():
            scatter(0, GROUP)

        @pl.when(b == GROUP + HALF - 1)
        def _():
            read(GROUP, HALF, 1, 0)

        @pl.when(b == GROUP + HALF)
        def _():
            exchange(send1, recv1, 0, 1)

        @pl.when(b == GROUP + HALF + 3)
        def _():
            gather(0)

        @pl.when(b == GROUP + HALF + 4)
        def _():
            exchange(send2, recv2, 0, 2)

        @pl.when(b == M - END - 1)
        def _():
            read(GROUP + HALF, HALF - END, 1, HALF * R)
            send_sums(1)

        @pl.when(b == M - 1)
        def _():
            read_end()

        @pl.when(b == M)
        def _():
            scatter(1, GROUP - END)
            exchange(send1, recv1, 1, 1)

        @pl.when(b == M + 1)
        def _():
            end_logs()

        @pl.when(b == M + 2)
        def _():
            gather(1)
            exchange(send2, recv2, 1, 2)

        return carry

    lax.fori_loop(0, M + MAX_LAG + 3, tick, 0)

    end_coeffs, end_shap = end_result()

    for g in range(N_GROUPS):
        whole(recv2.at[pl.ds(0, 15)], tail_recv.at[2, g]).wait_recv()
    coeffs = jnp.concatenate([recv2[:, 0], recv2[:, 1]], axis=-1)
    coeffs = jnp.concatenate([coeffs[: M - END], end_coeffs], axis=0)
    upper = lax.broadcasted_iota(jnp.int32, (M, R, CANDS), 1) >= 4
    lower = jnp.concatenate([coeffs[:, 4:], coeffs[:, :4]], axis=1)
    coeffs = coeffs - jnp.where(upper, lower, 0.0)
    for bit in range(5):
        step = 1 << bit
        pairs = coeffs.reshape(M // (2 * step), 2, step, R, CANDS)
        coeffs = jnp.concatenate(
            [pairs[:, :1], pairs[:, 1:] - pairs[:, :1]], axis=1
        ).reshape(M, R, CANDS)
    out_ref[:, 0] = coeffs[:, :4]
    out_ref[:, 1] = coeffs[:, 4:]
    shap = jnp.sum(recv2[:, 2].reshape(N_GROUPS, COALS, 8, 128), axis=0)
    shap = (shap + end_shap)[:GROUPS]
    shap_ref[:, :, :128] = shap[:, :4]
    shap_ref[:, :, 128:] = shap[:, 4:]

    waits = [
        (sums, 15 * (N_GROUPS + 1)),
        (send1, 15 * N_GROUPS),
        (send2, 15 * N_GROUPS),
        (ends, 15),
        (lines, 15),
    ]
    for kind, (ref, count) in enumerate(waits):
        whole(ref.at[pl.ds(0, count)], tail_send.at[kind]).wait_send()

    @pl.when(l < LAST)
    def _():
        for b in range(M - DEPTH, M):
            whole(rows.at[b], chain_send.at[b % DEPTH]).wait_send()

    @pl.when(y > 1)
    def _():
        whole(fin, fin_send.at[0]).wait_send()

    @pl.when(y == 1)
    def _():
        whole(fin.at[pl.ds(0, LATE)], fin_send.at[0]).wait_send()

    @pl.when(y == 3)
    def _():
        whole(fin.at[pl.ds(LATE, M - LATE)], fin_send.at[3]).wait_send()

    @pl.when((l == 15) | (l == 11))
    def _():
        whole(fin, fin_send.at[1]).wait_send()

    @pl.when(l == 15)
    def _():
        whole(fin, fin_send.at[2]).wait_send()


def per_device(
    base_rows,
    group_out,
    pre_gain,
    w_query,
    w_key,
    w_value,
    w_out,
    post_gain,
    key_cache,
    value_cache,
    final_gain,
    answer_rows,
):
    cosine, sine = rope_rows()
    vmem = pl.BlockSpec(memory_space=pltpu.VMEM)
    hbm = pl.BlockSpec(memory_space=pl.ANY)
    exchange = pltpu.VMEM((N_GROUPS * COALS, 3, 8, 128), f32)
    coeffs, shapley = pl.pallas_call(
        kernel,
        out_shape=(
            jax.ShapeDtypeStruct((M, 2, 4, CANDS), f32),
            jax.ShapeDtypeStruct((GROUPS, 4, CANDS), f32),
        ),
        in_specs=[vmem] * 7 + [hbm] * 7,
        out_specs=(vmem, vmem),
        scratch_shapes=[
            pltpu.VMEM((D, 512), bf16),
            pltpu.VMEM((256, D), bf16),
            pltpu.VMEM((PREFIX, HEAD), bf16),
            pltpu.VMEM((HEAD, PREFIX), bf16),
            pltpu.VMEM((PREFIX, HEAD), bf16),
            pltpu.VMEM((CANDS, D), bf16),
            pltpu.VMEM((D, CANDS), bf16),
            pltpu.VMEM((GROUPS, R, D), f32),
            pltpu.VMEM((M, R, D), f32),
            pltpu.VMEM((M, R, D), f32),
            pltpu.VMEM((N_GROUPS, G_ROWS, CANDS), f32),
            pltpu.VMEM(((N_GROUPS + 1) * SECTIONS, 8, 128), f32),
            exchange,
            exchange,
            exchange,
            exchange,
            pltpu.VMEM((COALS, E_ROWS, CANDS), f32),
            pltpu.VMEM((COALS, 8, 128), f32),
            pltpu.SemaphoreType.DMA((7,)),
            pltpu.SemaphoreType.DMA((M, CHUNKS)),
            pltpu.SemaphoreType.DMA((DEPTH,)),
            pltpu.SemaphoreType.DMA((M, FIN_CHUNKS)),
            pltpu.SemaphoreType.DMA((4,)),
            pltpu.SemaphoreType.DMA((5,)),
            pltpu.SemaphoreType.DMA((3, N_GROUPS + 1)),
        ],
        compiler_params=pltpu.CompilerParams(
            collective_id=0, has_side_effects=True, vmem_limit_bytes=58 << 20
        ),
    )(
        base_rows,
        group_out,
        pre_gain,
        post_gain,
        final_gain,
        jnp.asarray(cosine),
        jnp.asarray(sine),
        w_query[0],
        w_key[0],
        w_value[0],
        w_out[0],
        key_cache[0],
        value_cache[0],
        answer_rows,
    )
    return coeffs.reshape(64, 4, CANDS), shapley


def solution(mesh):
    placed = (
        P(),
        P(),
        P("section", None),
        P("section", None, None),
        P("section", None, None),
        P("section", None, None),
        P("section", None, None),
        P("section", None),
        P("section", None, None),
        P("section", None, None),
        P(),
        P("section", None),
    )
    return jax.shard_map(
        per_device,
        mesh=mesh,
        in_specs=placed,
        out_specs=(P("coal", None, "section"), P(None, None, "section")),
        check_vma=False,
    )
```

```python
import functools

import jax
import jax.numpy as jnp
import numpy as np
from jax import lax
from jax.experimental import pallas as pl
from jax.experimental.pallas import tpu as pltpu
from jax.sharding import PartitionSpec as P

f32, bf16 = jnp.float32, jnp.bfloat16
MESH = pl.DeviceIdType.MESH

D = 4608
HEAD = 128
PREFIX = 2048
GROUPS = 10
SECTIONS = 16
COALS = 16
R = 8
M = 32
CANDS = 256
EPS = 1e-6
LAST = SECTIONS - 1
CHUNKS = 4
DEPTH = 3
WIDE = D // CHUNKS
GROUP = 16
HALF = GROUP // 2
N_GROUPS = M // GROUP
G_ROWS = GROUP * R
END = 2
E_ROWS = END * R
HOP = 60
MAX_LAG = 40
FAR_FIRST = (8, 7, 9, 6, 10, 5, 11, 4, 12, 3, 13, 2, 14, 1, 15)
FIN_CHUNKS = 4
FIN_WIDE = D // FIN_CHUNKS
LATE = 26


def rope_rows():
    half = HEAD // 2
    places = PREFIX + np.arange(R) % 4
    inverse = 10000.0 ** (-2.0 * np.arange(half) / HEAD)
    angles = places[:, None] * inverse[None, :]
    cosine, sine = np.cos(angles), np.sin(angles)
    return (
        np.concatenate([cosine, cosine], axis=1).astype(np.float32),
        np.concatenate([-sine, sine], axis=1).astype(np.float32),
    )


def split2(x):
    high = x.astype(bf16).astype(f32)
    return jnp.concatenate([high, x - high], axis=0).astype(bf16)


def fold(y):
    half = y.shape[0] // 2
    return y[:half] + y[half:]


def dot(left, right):
    return jnp.dot(left, right, preferred_element_type=f32)


def attention(y, kt_ref, v_ref, cosine, sine):
    rows = y.shape[0]

    def rotated(z):
        return z * cosine + pltpu.roll(z, HEAD // 2, 1) * sine

    q = jnp.concatenate([rotated(y[:, :128]), rotated(y[:, 128:256])], axis=0)
    q = q * (1.0 / 600.0)
    k = rotated(y[:, 256:384])
    v = y[:, 384:512]
    p = jnp.exp(50.0 * jnp.tanh(fold(dot(split2(q), kt_ref[...]))))
    mixed = fold(dot(split2(p), v_ref[...]))
    total = jnp.sum(p, axis=-1, keepdims=True)
    place = lax.broadcasted_iota(jnp.int32, (2 * rows, 1), 0) % 4
    for back in range(4):
        k_back = pltpu.roll(k, back, 0) if back else k
        v_back = pltpu.roll(v, back, 0) if back else v
        score = jnp.sum(
            q * jnp.concatenate([k_back, k_back], axis=0), axis=-1, keepdims=True
        )
        weight = jnp.where(place >= back, jnp.exp(50.0 * jnp.tanh(score)), 0.0)
        total = total + weight
        mixed = mixed + weight * jnp.concatenate([v_back, v_back], axis=0)
    attended = mixed / total
    return jnp.concatenate([attended[:rows], attended[rows:]], axis=1)


def shapley_weights(shape, ident_of):
    row = lax.broadcasted_iota(jnp.int32, shape, 0)
    column = lax.broadcasted_iota(jnp.int32, shape, 1)
    group = row // 8
    ident = ident_of(column)
    size = jnp.zeros(shape, jnp.int32)
    for g in range(GROUPS):
        size = size + ((ident >> g) & 1)
    has = (ident >> group) & 1
    others = size - has
    weight = jnp.zeros(shape, f32)
    fact = [1.0]
    for n in range(1, GROUPS + 1):
        fact.append(fact[-1] * n)
    for n in range(GROUPS):
        value = fact[n] * fact[GROUPS - 1 - n] / fact[GROUPS]
        weight = jnp.where(others == n, value, weight)
    weight = jnp.where(has == 1, weight, -weight)
    return jnp.where((row % 4 == column % 4) & (group < GROUPS), weight, 0.0)


def kernel(
    base_ref,
    group_ref,
    pre_ref,
    post_ref,
    fin_gain_ref,
    cos_ref,
    sin_ref,
    wq_hbm,
    wk_hbm,
    wv_hbm,
    wo_hbm,
    key_hbm,
    val_hbm,
    ans_hbm,
    out_ref,
    shap_ref,
    w,
    wo,
    key,
    kt,
    val,
    ans,
    ans_t,
    groups,
    rows,
    fin,
    capped,
    sums,
    send1,
    recv1,
    send2,
    recv2,
    ends,
    lines,
    init_sem,
    chain_recv,
    chain_send,
    fin_recv,
    fin_send,
    tail_send,
    tail_recv,
):
    l = lax.axis_index("section")
    c = lax.axis_index("coal")
    y = lax.rem(l, 4)
    x = l // 4

    loads = [
        (wq_hbm, w.at[:, pl.ds(0, 256)]),
        (wk_hbm, w.at[:, pl.ds(256, 128)]),
        (wv_hbm, w.at[:, pl.ds(384, 128)]),
        (key_hbm, key),
        (val_hbm, val),
        (wo_hbm, wo),
        (ans_hbm, ans),
    ]
    loads = [
        pltpu.make_async_copy(a, b, init_sem.at[i]) for i, (a, b) in enumerate(loads)
    ]
    for load in loads:
        load.start()

    barrier = pltpu.get_barrier_semaphore()

    def greet(device):
        pl.semaphore_signal(barrier, inc=1, device_id=device, device_id_type=MESH)

    def greet_coal():
        for k in range(1, COALS):
            greet((l, lax.rem(c + k, COALS)))

    @pl.when(l == 0)
    def _():
        greet_coal()

    for k in range(SECTIONS):

        @pl.when(l != k)
        def _():
            greet((k, c))

    @pl.when(l != 0)
    def _():
        greet_coal()

    @pl.when(l == 0)
    def _():
        g = group_ref[...].astype(f32)
        groups[...] = jnp.concatenate([g, g], axis=1)

    for load in loads[:-1]:
        load.wait()
    kt[...] = key[...].T

    def turn_answers():
        loads[-1].wait()

        def turn(i, carry):
            at = pl.multiple_of(i * 128, 128)
            ans_t[pl.ds(at, 128), :] = ans[:, pl.ds(at, 128)].T
            return carry

        lax.fori_loop(0, D // 128, turn, 0)

    @pl.when(l > 0)
    def _():
        turn_answers()

    pl.semaphore_wait(barrier, 30)

    def part(j):
        return pl.ds(j * WIDE, WIDE)

    def chain_copy(b, j):
        return pltpu.make_async_remote_copy(
            src_ref=rows.at[b, :, part(j)],
            dst_ref=rows.at[b, :, part(j)],
            send_sem=chain_send.at[lax.rem(b, DEPTH)],
            recv_sem=chain_recv.at[b, j],
            device_id=(lax.rem(l + 1, SECTIONS), c),
            device_id_type=MESH,
        )

    def fin_copy(b, f, child, sem):
        piece = fin.at[b, :, pl.ds(f * FIN_WIDE, FIN_WIDE)]
        return pltpu.make_async_remote_copy(
            src_ref=piece,
            dst_ref=piece,
            send_sem=fin_send.at[sem],
            recv_sem=fin_recv.at[b, f],
            device_id=(child, c),
            device_id_type=MESH,
        )

    def spread(b, f):
        @pl.when((l == 15) | (l == 11))
        def _():
            fin_copy(b, f, l - 4, 1).start()

        @pl.when(l == 15)
        def _():
            fin_copy(b, f, 3, 2).start()

        @pl.when((y > 1) | ((y == 1) & (b < LATE)))
        def _():
            fin_copy(b, f, l - 1, 0).start()

        @pl.when((y == 3) & (b >= LATE))
        def _():
            fin_copy(b, f, l - 3, 3).start()

    def whole(ref, sem):
        return pltpu.make_async_remote_copy(
            src_ref=ref,
            dst_ref=ref,
            send_sem=sem,
            recv_sem=sem,
            device_id=(l, c),
            device_id_type=MESH,
        )

    def work(b):
        @pl.when(l == 0)
        def _():
            ident = c * 64 + 2 * b + lax.broadcasted_iota(jnp.int32, (R, 1), 0) // 4
            b32 = base_ref[...].astype(f32)
            acc = jnp.concatenate([b32, b32], axis=0)
            for g in range(GROUPS):
                acc = acc + ((ident >> g) & 1).astype(f32) * groups[g]
            rows[b] = acc

        square = jnp.zeros((R, 1), f32)
        mixed = jnp.zeros((2 * R, 512), f32)
        for j in range(CHUNKS):

            @pl.when(l > 0)
            def _():
                chain_copy(b, j).wait_recv()

            piece = rows[b, :, part(j)]
            square = square + jnp.sum(piece * piece, axis=-1, keepdims=True)
            mixed = mixed + dot(split2(piece * pre_ref[:, part(j)]), w[part(j), :])
        inv = lax.rsqrt(square * (1.0 / D) + EPS)
        attended = attention(fold(mixed) * inv, kt, val, cos_ref[...], sin_ref[...])
        proj = fold(dot(split2(attended), wo[...]))
        scale = lax.rsqrt(jnp.mean(proj * proj, axis=-1, keepdims=True) + EPS)

        @pl.when((l < LAST) & (b >= DEPTH))
        def _():
            whole(rows.at[b - DEPTH], chain_send.at[lax.rem(b, DEPTH)]).wait_send()

        @pl.when(l < LAST)
        def _():
            for j in range(CHUNKS):
                rows[b, :, part(j)] = (
                    rows[b, :, part(j)]
                    + proj[:, j * WIDE : (j + 1) * WIDE] * scale * post_ref[:, part(j)]
                )
                chain_copy(b, j).start()

        @pl.when(l == LAST)
        def _():
            new = rows[b] + proj * scale * post_ref[...]
            inv = lax.rsqrt(jnp.mean(new * new, axis=-1, keepdims=True) + EPS)
            fin[b] = new * inv * fin_gain_ref[...].reshape(1, D)
            for f in range(FIN_CHUNKS):
                spread(b, f)

    def eye(shape):
        return lax.broadcasted_iota(jnp.int32, shape, len(shape) - 2) == (
            lax.broadcasted_iota(jnp.int32, shape, len(shape) - 1)
        )

    def score(first, count):
        block = fin[pl.ds(first, count)].reshape(count * R, D)
        logits = fold(dot(split2(block), ans_t[...]))
        return 30.0 * jnp.tanh(logits * (1.0 / 30.0))

    def line_of(values, lane):
        n = values.shape[0]
        column = jnp.sum(jnp.exp(values), axis=-1, keepdims=True)
        here = lax.broadcasted_iota(jnp.int32, (n, 128), 0) + lane
        here = here == lax.broadcasted_iota(jnp.int32, (n, 128), 1)
        line = jnp.sum(jnp.where(here, column, 0.0), axis=0, keepdims=True)
        return jnp.broadcast_to(line, (8, 128))

    def read(first, count, g, lane):
        values = score(first, count)
        capped[g, pl.ds(lane, count * R)] = values
        mine = g * SECTIONS + l
        line = line_of(values, lane)
        sums[mine] = line if lane == 0 else sums[mine] + line

    def send_sums(slot):
        mine = slot * SECTIONS + l
        for k in FAR_FIRST:
            pltpu.make_async_remote_copy(
                src_ref=sums.at[mine],
                dst_ref=sums.at[mine],
                send_sem=tail_send.at[0],
                recv_sem=tail_recv.at[0, slot],
                device_id=(lax.rem(l + k, SECTIONS), c),
                device_id_type=MESH,
            ).start()

    def read_end():
        values = score(M - END, END)
        ends[c] = values
        sums[N_GROUPS * SECTIONS + l] = line_of(values, 0)
        send_sums(N_GROUPS)
        for k in FAR_FIRST:
            end_copy(lax.rem(c + k, COALS)).start()

    def end_copy(peer):
        return pltpu.make_async_remote_copy(
            src_ref=ends.at[c],
            dst_ref=ends.at[c],
            send_sem=tail_send.at[3],
            recv_sem=tail_recv.at[1, N_GROUPS],
            device_id=(l, peer),
            device_id_type=MESH,
        )

    def logs_of(slot):
        whole(sums.at[pl.ds(0, 15)], tail_recv.at[0, slot]).wait_recv()
        return jnp.log(jnp.sum(sums[pl.ds(slot * SECTIONS, SECTIONS)], axis=0))

    def end_logs():
        lines[c] = logs_of(N_GROUPS)
        for k in FAR_FIRST:
            pltpu.make_async_remote_copy(
                src_ref=lines.at[c],
                dst_ref=lines.at[c],
                send_sem=tail_send.at[4],
                recv_sem=tail_recv.at[2, N_GROUPS],
                device_id=(l, lax.rem(c + k, COALS)),
                device_id_type=MESH,
            ).start()

    def end_result():
        def ident(column):
            return column // E_ROWS * 64 + (64 - 2 * END) + lax.rem(column, E_ROWS) // 4

        weights = shapley_weights((16 * 8, COALS * E_ROWS), ident)
        signs = []
        for other in range(COALS):
            sign = 1
            for bit in range(4):
                has = (c >> bit) & 1
                sign = sign * (has if (other >> bit) & 1 else 1 - 2 * has)
            signs.append(sign.astype(f32))
        whole(ends.at[pl.ds(0, 15)], tail_recv.at[1, N_GROUPS]).wait_recv()
        whole(lines.at[pl.ds(0, 15)], tail_recv.at[2, N_GROUPS]).wait_recv()
        logs = jnp.sum(
            jnp.where(eye((COALS, E_ROWS, 128)), lines[:, 0:1, :], 0.0),
            axis=-1,
            keepdims=True,
        )
        values = ends[...] - logs
        coeffs = signs[0] * values[0]
        for other in range(1, COALS):
            coeffs = coeffs + signs[other] * values[other]
        shap = jnp.dot(
            weights,
            values.reshape(COALS * E_ROWS, CANDS),
            preferred_element_type=f32,
            precision=lax.Precision.HIGHEST,
        )
        return coeffs.reshape(END, R, CANDS), halves(shap)

    def halves(shap):
        shap = shap.reshape(16, 8, CANDS)
        low = lax.broadcasted_iota(jnp.int32, (16, 8, 128), 1) < 4
        return jnp.where(low, shap[:, :, :128], shap[:, :, 128:])

    def exchange(src, dst, g, kind):
        for k in FAR_FIRST:
            peer = lax.rem(c + k, COALS)
            pltpu.make_async_remote_copy(
                src_ref=src.at[g * COALS + peer],
                dst_ref=dst.at[g * COALS + c],
                send_sem=tail_send.at[kind],
                recv_sem=tail_recv.at[kind, g],
                device_id=(l, peer),
                device_id_type=MESH,
            ).start()
        dst[g * COALS + c] = src[g * COALS + c]

    def scatter(g, count):
        n = count * R
        column = jnp.sum(
            jnp.where(eye((n, 128)), logs_of(g)[0:1], 0.0), axis=1, keepdims=True
        )
        values = capped[g, pl.ds(0, n)] - column
        first = c * 64 + g * (2 * GROUP)
        shap = jnp.dot(
            shapley_weights((16 * 8, n), lambda column: first + column // 4),
            values,
            preferred_element_type=f32,
            precision=lax.Precision.HIGHEST,
        )
        values = values.reshape(count, R, CANDS)
        for h in range(2):
            send1[pl.ds(g * COALS, count), h] = values[:, :, 128 * h : 128 * h + 128]
            if count < GROUP:
                send1[pl.ds(g * COALS + count, GROUP - count), h] = jnp.zeros(
                    (GROUP - count, 8, 128), f32
                )
        send1[pl.ds(g * COALS, COALS), 2] = halves(shap)

    def gather(g):
        whole(recv1.at[pl.ds(0, 15)], tail_recv.at[1, g]).wait_recv()
        slots = pl.ds(g * COALS, COALS)
        got = recv1[slots, 0:2]
        for bit in range(4):
            step = 1 << bit
            pairs = got.reshape(COALS // (2 * step), 2, step, 2, 8, 128)
            got = jnp.concatenate(
                [pairs[:, :1], pairs[:, 1:] - pairs[:, :1]], axis=1
            ).reshape(COALS, 2, 8, 128)
        total = jnp.sum(recv1[slots, 2], axis=0)
        send2[slots, 0:2] = got
        send2[slots, 2] = jnp.broadcast_to(total[None], (COALS, 8, 128))

    away = jnp.where(x == 3, 0, jnp.where(x == 1, 2, 1)) + 3 - y
    lag = (HOP * (LAST - l) + 10 + 45 * away + 32) // 33
    lag = jnp.where(l == LAST, 0, jnp.where(l == 0, MAX_LAG, lag))

    def tick(t, carry):
        @pl.when(t < M)
        def _():
            work(t)

        @pl.when((l == 0) & (t == M))
        def _():
            turn_answers()

        b = t - lag

        @pl.when((l < LAST) & (b >= 0) & (b < M))
        def _():
            for f in range(FIN_CHUNKS):
                fin_copy(b, f, l, 0).wait_recv()
                spread(b, f)

        @pl.when(b == HALF - 1)
        def _():
            read(0, HALF, 0, 0)

        @pl.when(b == GROUP - 1)
        def _():
            read(HALF, HALF, 0, HALF * R)

        @pl.when(b == GROUP)
        def _():
            send_sums(0)

        @pl.when(b == GROUP + 6)
        def _():
            scatter(0, GROUP)

        @pl.when(b == GROUP + HALF - 1)
        def _():
            read(GROUP, HALF, 1, 0)

        @pl.when(b == GROUP + HALF)
        def _():
            exchange(send1, recv1, 0, 1)

        @pl.when(b == GROUP + HALF + 3)
        def _():
            gather(0)

        @pl.when(b == GROUP + HALF + 4)
        def _():
            exchange(send2, recv2, 0, 2)

        @pl.when(b == M - END - 1)
        def _():
            read(GROUP + HALF, HALF - END, 1, HALF * R)
            send_sums(1)

        @pl.when(b == M - 1)
        def _():
            scatter(1, GROUP - END)
            exchange(send1, recv1, 1, 1)
            read_end()

        @pl.when(b == M + 1)
        def _():
            end_logs()

        @pl.when(b == M + 2)
        def _():
            gather(1)
            exchange(send2, recv2, 1, 2)

        return carry

    lax.fori_loop(0, M + MAX_LAG + 3, tick, 0)

    end_coeffs, end_shap = end_result()

    for g in range(N_GROUPS):
        whole(recv2.at[pl.ds(0, 15)], tail_recv.at[2, g]).wait_recv()
    coeffs = jnp.concatenate([recv2[:, 0], recv2[:, 1]], axis=-1)
    coeffs = jnp.concatenate([coeffs[: M - END], end_coeffs], axis=0)
    upper = lax.broadcasted_iota(jnp.int32, (M, R, CANDS), 1) >= 4
    lower = jnp.concatenate([coeffs[:, 4:], coeffs[:, :4]], axis=1)
    coeffs = coeffs - jnp.where(upper, lower, 0.0)
    for bit in range(5):
        step = 1 << bit
        pairs = coeffs.reshape(M // (2 * step), 2, step, R, CANDS)
        coeffs = jnp.concatenate(
            [pairs[:, :1], pairs[:, 1:] - pairs[:, :1]], axis=1
        ).reshape(M, R, CANDS)
    out_ref[:, 0] = coeffs[:, :4]
    out_ref[:, 1] = coeffs[:, 4:]
    shap = jnp.sum(recv2[:, 2].reshape(N_GROUPS, COALS, 8, 128), axis=0)
    shap = (shap + end_shap)[:GROUPS]
    shap_ref[:, :, :128] = shap[:, :4]
    shap_ref[:, :, 128:] = shap[:, 4:]

    waits = [
        (sums, 15 * (N_GROUPS + 1)),
        (send1, 15 * N_GROUPS),
        (send2, 15 * N_GROUPS),
        (ends, 15),
        (lines, 15),
    ]
    for kind, (ref, count) in enumerate(waits):
        whole(ref.at[pl.ds(0, count)], tail_send.at[kind]).wait_send()

    @pl.when(l < LAST)
    def _():
        for b in range(M - DEPTH, M):
            whole(rows.at[b], chain_send.at[b % DEPTH]).wait_send()

    @pl.when(y > 1)
    def _():
        whole(fin, fin_send.at[0]).wait_send()

    @pl.when(y == 1)
    def _():
        whole(fin.at[pl.ds(0, LATE)], fin_send.at[0]).wait_send()

    @pl.when(y == 3)
    def _():
        whole(fin.at[pl.ds(LATE, M - LATE)], fin_send.at[3]).wait_send()

    @pl.when((l == 15) | (l == 11))
    def _():
        whole(fin, fin_send.at[1]).wait_send()

    @pl.when(l == 15)
    def _():
        whole(fin, fin_send.at[2]).wait_send()


def per_device(
    base_rows,
    group_out,
    pre_gain,
    w_query,
    w_key,
    w_value,
    w_out,
    post_gain,
    key_cache,
    value_cache,
    final_gain,
    answer_rows,
):
    cosine, sine = rope_rows()
    vmem = pl.BlockSpec(memory_space=pltpu.VMEM)
    hbm = pl.BlockSpec(memory_space=pl.ANY)
    exchange = pltpu.VMEM((N_GROUPS * COALS, 3, 8, 128), f32)
    coeffs, shapley = pl.pallas_call(
        kernel,
        out_shape=(
            jax.ShapeDtypeStruct((M, 2, 4, CANDS), f32),
            jax.ShapeDtypeStruct((GROUPS, 4, CANDS), f32),
        ),
        in_specs=[vmem] * 7 + [hbm] * 7,
        out_specs=(vmem, vmem),
        scratch_shapes=[
            pltpu.VMEM((D, 512), bf16),
            pltpu.VMEM((256, D), bf16),
            pltpu.VMEM((PREFIX, HEAD), bf16),
            pltpu.VMEM((HEAD, PREFIX), bf16),
            pltpu.VMEM((PREFIX, HEAD), bf16),
            pltpu.VMEM((CANDS, D), bf16),
            pltpu.VMEM((D, CANDS), bf16),
            pltpu.VMEM((GROUPS, R, D), f32),
            pltpu.VMEM((M, R, D), f32),
            pltpu.VMEM((M, R, D), f32),
            pltpu.VMEM((N_GROUPS, G_ROWS, CANDS), f32),
            pltpu.VMEM(((N_GROUPS + 1) * SECTIONS, 8, 128), f32),
            exchange,
            exchange,
            exchange,
            exchange,
            pltpu.VMEM((COALS, E_ROWS, CANDS), f32),
            pltpu.VMEM((COALS, 8, 128), f32),
            pltpu.SemaphoreType.DMA((7,)),
            pltpu.SemaphoreType.DMA((M, CHUNKS)),
            pltpu.SemaphoreType.DMA((DEPTH,)),
            pltpu.SemaphoreType.DMA((M, FIN_CHUNKS)),
            pltpu.SemaphoreType.DMA((4,)),
            pltpu.SemaphoreType.DMA((5,)),
            pltpu.SemaphoreType.DMA((3, N_GROUPS + 1)),
        ],
        compiler_params=pltpu.CompilerParams(
            collective_id=0, has_side_effects=True, vmem_limit_bytes=58 << 20
        ),
    )(
        base_rows,
        group_out,
        pre_gain,
        post_gain,
        final_gain,
        jnp.asarray(cosine),
        jnp.asarray(sine),
        w_query[0],
        w_key[0],
        w_value[0],
        w_out[0],
        key_cache[0],
        value_cache[0],
        answer_rows,
    )
    return coeffs.reshape(64, 4, CANDS), shapley


def solution(mesh):
    placed = (
        P(),
        P(),
        P("section", None),
        P("section", None, None),
        P("section", None, None),
        P("section", None, None),
        P("section", None, None),
        P("section", None),
        P("section", None, None),
        P("section", None, None),
        P(),
        P("section", None),
    )
    return jax.shard_map(
        per_device,
        mesh=mesh,
        in_specs=placed,
        out_specs=(P("coal", None, "section"), P(None, None, "section")),
        check_vma=False,
    )
```

```python
import functools

import jax
import jax.numpy as jnp
import numpy as np
from jax import lax
from jax.experimental import pallas as pl
from jax.experimental.pallas import tpu as pltpu
from jax.sharding import PartitionSpec as P

f32, bf16 = jnp.float32, jnp.bfloat16
MESH = pl.DeviceIdType.MESH

D = 4608
HEAD = 128
PREFIX = 2048
GROUPS = 10
SECTIONS = 16
COALS = 16
R = 8
M = 32
CANDS = 256
EPS = 1e-6
LAST = SECTIONS - 1
CHUNKS = 4
DEPTH = 3
WIDE = D // CHUNKS
GROUP = 16
HALF = GROUP // 2
N_GROUPS = M // GROUP
G_ROWS = GROUP * R
END = 2
E_ROWS = END * R
HOP = 60
MAX_LAG = 40
FAR_FIRST = (8, 7, 9, 6, 10, 5, 11, 4, 12, 3, 13, 2, 14, 1, 15)
FIN_CHUNKS = 4
FIN_WIDE = D // FIN_CHUNKS
LATE = 26


def rope_rows():
    half = HEAD // 2
    places = PREFIX + np.arange(R) % 4
    inverse = 10000.0 ** (-2.0 * np.arange(half) / HEAD)
    angles = places[:, None] * inverse[None, :]
    cosine, sine = np.cos(angles), np.sin(angles)
    return (
        np.concatenate([cosine, cosine], axis=1).astype(np.float32),
        np.concatenate([-sine, sine], axis=1).astype(np.float32),
    )


def split2(x):
    high = x.astype(bf16).astype(f32)
    return jnp.concatenate([high, x - high], axis=0).astype(bf16)


def fold(y):
    half = y.shape[0] // 2
    return y[:half] + y[half:]


def dot(left, right):
    return jnp.dot(left, right, preferred_element_type=f32)


def attention(y, kt_ref, v_ref, cosine, sine):
    rows = y.shape[0]

    def rotated(z):
        return z * cosine + pltpu.roll(z, HEAD // 2, 1) * sine

    q = jnp.concatenate([rotated(y[:, :128]), rotated(y[:, 128:256])], axis=0)
    q = q * (1.0 / 600.0)
    k = rotated(y[:, 256:384])
    v = y[:, 384:512]
    p = jnp.exp(50.0 * jnp.tanh(fold(dot(split2(q), kt_ref[...]))))
    mixed = fold(dot(split2(p), v_ref[...]))
    total = jnp.sum(p, axis=-1, keepdims=True)
    place = lax.broadcasted_iota(jnp.int32, (2 * rows, 1), 0) % 4
    for back in range(4):
        k_back = pltpu.roll(k, back, 0) if back else k
        v_back = pltpu.roll(v, back, 0) if back else v
        score = jnp.sum(
            q * jnp.concatenate([k_back, k_back], axis=0), axis=-1, keepdims=True
        )
        weight = jnp.where(place >= back, jnp.exp(50.0 * jnp.tanh(score)), 0.0)
        total = total + weight
        mixed = mixed + weight * jnp.concatenate([v_back, v_back], axis=0)
    attended = mixed / total
    return jnp.concatenate([attended[:rows], attended[rows:]], axis=1)


def shapley_weights(shape, ident_of):
    row = lax.broadcasted_iota(jnp.int32, shape, 0)
    column = lax.broadcasted_iota(jnp.int32, shape, 1)
    group = row // 8
    ident = ident_of(column)
    size = jnp.zeros(shape, jnp.int32)
    for g in range(GROUPS):
        size = size + ((ident >> g) & 1)
    has = (ident >> group) & 1
    others = size - has
    weight = jnp.zeros(shape, f32)
    fact = [1.0]
    for n in range(1, GROUPS + 1):
        fact.append(fact[-1] * n)
    for n in range(GROUPS):
        value = fact[n] * fact[GROUPS - 1 - n] / fact[GROUPS]
        weight = jnp.where(others == n, value, weight)
    weight = jnp.where(has == 1, weight, -weight)
    return jnp.where((row % 4 == column % 4) & (group < GROUPS), weight, 0.0)


def kernel(
    base_ref,
    group_ref,
    pre_ref,
    post_ref,
    fin_gain_ref,
    cos_ref,
    sin_ref,
    wq_hbm,
    wk_hbm,
    wv_hbm,
    wo_hbm,
    key_hbm,
    val_hbm,
    ans_hbm,
    out_ref,
    shap_ref,
    w,
    wo,
    key,
    kt,
    val,
    ans,
    ans_t,
    groups,
    rows,
    fin,
    capped,
    sums,
    send1,
    recv1,
    send2,
    recv2,
    ends,
    lines,
    init_sem,
    chain_recv,
    chain_send,
    fin_recv,
    fin_send,
    tail_send,
    tail_recv,
):
    l = lax.axis_index("section")
    c = lax.axis_index("coal")
    y = lax.rem(l, 4)
    x = l // 4

    loads = [
        (wq_hbm, w.at[:, pl.ds(0, 256)]),
        (wk_hbm, w.at[:, pl.ds(256, 128)]),
        (wv_hbm, w.at[:, pl.ds(384, 128)]),
        (key_hbm, key),
        (val_hbm, val),
        (wo_hbm, wo),
        (ans_hbm, ans),
    ]
    loads = [
        pltpu.make_async_copy(a, b, init_sem.at[i]) for i, (a, b) in enumerate(loads)
    ]
    for load in loads[:-1]:
        load.start()

    barrier = pltpu.get_barrier_semaphore()

    def greet(device):
        pl.semaphore_signal(barrier, inc=1, device_id=device, device_id_type=MESH)

    def greet_coal():
        for k in range(1, COALS):
            greet((l, lax.rem(c + k, COALS)))

    @pl.when(l == 0)
    def _():
        greet_coal()

    for k in range(SECTIONS):

        @pl.when(l != k)
        def _():
            greet((k, c))

    @pl.when(l != 0)
    def _():
        greet_coal()

    @pl.when(l == 0)
    def _():
        g = group_ref[...].astype(f32)
        groups[...] = jnp.concatenate([g, g], axis=1)

    for load in loads[:-1]:
        load.wait()
    loads[-1].start()
    kt[...] = key[...].T

    def turn_answers():
        loads[-1].wait()

        def turn(i, carry):
            at = pl.multiple_of(i * 128, 128)
            ans_t[pl.ds(at, 128), :] = ans[:, pl.ds(at, 128)].T
            return carry

        lax.fori_loop(0, D // 128, turn, 0)

    @pl.when(l > 0)
    def _():
        turn_answers()

    pl.semaphore_wait(barrier, 30)

    def part(j):
        return pl.ds(j * WIDE, WIDE)

    def chain_copy(b, j):
        return pltpu.make_async_remote_copy(
            src_ref=rows.at[b, :, part(j)],
            dst_ref=rows.at[b, :, part(j)],
            send_sem=chain_send.at[lax.rem(b, DEPTH)],
            recv_sem=chain_recv.at[b, j],
            device_id=(lax.rem(l + 1, SECTIONS), c),
            device_id_type=MESH,
        )

    def fin_copy(b, f, child, sem):
        piece = fin.at[b, :, pl.ds(f * FIN_WIDE, FIN_WIDE)]
        return pltpu.make_async_remote_copy(
            src_ref=piece,
            dst_ref=piece,
            send_sem=fin_send.at[sem],
            recv_sem=fin_recv.at[b, f],
            device_id=(child, c),
            device_id_type=MESH,
        )

    def spread(b, f):
        @pl.when((l == 15) | (l == 11))
        def _():
            fin_copy(b, f, l - 4, 1).start()

        @pl.when(l == 15)
        def _():
            fin_copy(b, f, 3, 2).start()

        @pl.when((y > 1) | ((y == 1) & (b < LATE)))
        def _():
            fin_copy(b, f, l - 1, 0).start()

        @pl.when((y == 3) & (b >= LATE))
        def _():
            fin_copy(b, f, l - 3, 3).start()

    def whole(ref, sem):
        return pltpu.make_async_remote_copy(
            src_ref=ref,
            dst_ref=ref,
            send_sem=sem,
            recv_sem=sem,
            device_id=(l, c),
            device_id_type=MESH,
        )

    def work(b):
        @pl.when(l == 0)
        def _():
            ident = c * 64 + 2 * b + lax.broadcasted_iota(jnp.int32, (R, 1), 0) // 4
            b32 = base_ref[...].astype(f32)
            acc = jnp.concatenate([b32, b32], axis=0)
            for g in range(GROUPS):
                acc = acc + ((ident >> g) & 1).astype(f32) * groups[g]
            rows[b] = acc

        square = jnp.zeros((R, 1), f32)
        mixed = jnp.zeros((2 * R, 512), f32)
        for j in range(CHUNKS):

            @pl.when(l > 0)
            def _():
                chain_copy(b, j).wait_recv()

            piece = rows[b, :, part(j)]
            square = square + jnp.sum(piece * piece, axis=-1, keepdims=True)
            mixed = mixed + dot(split2(piece * pre_ref[:, part(j)]), w[part(j), :])
        inv = lax.rsqrt(square * (1.0 / D) + EPS)
        attended = attention(fold(mixed) * inv, kt, val, cos_ref[...], sin_ref[...])
        proj = fold(dot(split2(attended), wo[...]))
        scale = lax.rsqrt(jnp.mean(proj * proj, axis=-1, keepdims=True) + EPS)

        @pl.when((l < LAST) & (b >= DEPTH))
        def _():
            whole(rows.at[b - DEPTH], chain_send.at[lax.rem(b, DEPTH)]).wait_send()

        @pl.when(l < LAST)
        def _():
            for j in range(CHUNKS):
                rows[b, :, part(j)] = (
                    rows[b, :, part(j)]
                    + proj[:, j * WIDE : (j + 1) * WIDE] * scale * post_ref[:, part(j)]
                )
                chain_copy(b, j).start()

        @pl.when(l == LAST)
        def _():
            new = rows[b] + proj * scale * post_ref[...]
            inv = lax.rsqrt(jnp.mean(new * new, axis=-1, keepdims=True) + EPS)
            fin[b] = new * inv * fin_gain_ref[...].reshape(1, D)
            for f in range(FIN_CHUNKS):
                spread(b, f)

    def eye(shape):
        return lax.broadcasted_iota(jnp.int32, shape, len(shape) - 2) == (
            lax.broadcasted_iota(jnp.int32, shape, len(shape) - 1)
        )

    def score(first, count):
        block = fin[pl.ds(first, count)].reshape(count * R, D)
        logits = fold(dot(split2(block), ans_t[...]))
        return 30.0 * jnp.tanh(logits * (1.0 / 30.0))

    def line_of(values, lane):
        n = values.shape[0]
        column = jnp.sum(jnp.exp(values), axis=-1, keepdims=True)
        here = lax.broadcasted_iota(jnp.int32, (n, 128), 0) + lane
        here = here == lax.broadcasted_iota(jnp.int32, (n, 128), 1)
        line = jnp.sum(jnp.where(here, column, 0.0), axis=0, keepdims=True)
        return jnp.broadcast_to(line, (8, 128))

    def read(first, count, g, lane):
        values = score(first, count)
        capped[g, pl.ds(lane, count * R)] = values
        mine = g * SECTIONS + l
        line = line_of(values, lane)
        sums[mine] = line if lane == 0 else sums[mine] + line

    def send_sums(slot):
        mine = slot * SECTIONS + l
        for k in FAR_FIRST:
            pltpu.make_async_remote_copy(
                src_ref=sums.at[mine],
                dst_ref=sums.at[mine],
                send_sem=tail_send.at[0],
                recv_sem=tail_recv.at[0, slot],
                device_id=(lax.rem(l + k, SECTIONS), c),
                device_id_type=MESH,
            ).start()

    def read_end():
        values = score(M - END, END)
        ends[c] = values
        sums[N_GROUPS * SECTIONS + l] = line_of(values, 0)
        send_sums(N_GROUPS)
        for k in FAR_FIRST:
            end_copy(lax.rem(c + k, COALS)).start()

    def end_copy(peer):
        return pltpu.make_async_remote_copy(
            src_ref=ends.at[c],
            dst_ref=ends.at[c],
            send_sem=tail_send.at[3],
            recv_sem=tail_recv.at[1, N_GROUPS],
            device_id=(l, peer),
            device_id_type=MESH,
        )

    def logs_of(slot):
        whole(sums.at[pl.ds(0, 15)], tail_recv.at[0, slot]).wait_recv()
        return jnp.log(jnp.sum(sums[pl.ds(slot * SECTIONS, SECTIONS)], axis=0))

    def end_logs():
        lines[c] = logs_of(N_GROUPS)
        for k in FAR_FIRST:
            pltpu.make_async_remote_copy(
                src_ref=lines.at[c],
                dst_ref=lines.at[c],
                send_sem=tail_send.at[4],
                recv_sem=tail_recv.at[2, N_GROUPS],
                device_id=(l, lax.rem(c + k, COALS)),
                device_id_type=MESH,
            ).start()

    def end_result():
        def ident(column):
            return column // E_ROWS * 64 + (64 - 2 * END) + lax.rem(column, E_ROWS) // 4

        weights = shapley_weights((16 * 8, COALS * E_ROWS), ident)
        signs = []
        for other in range(COALS):
            sign = 1
            for bit in range(4):
                has = (c >> bit) & 1
                sign = sign * (has if (other >> bit) & 1 else 1 - 2 * has)
            signs.append(sign.astype(f32))
        whole(ends.at[pl.ds(0, 15)], tail_recv.at[1, N_GROUPS]).wait_recv()
        whole(lines.at[pl.ds(0, 15)], tail_recv.at[2, N_GROUPS]).wait_recv()
        logs = jnp.sum(
            jnp.where(eye((COALS, E_ROWS, 128)), lines[:, 0:1, :], 0.0),
            axis=-1,
            keepdims=True,
        )
        values = ends[...] - logs
        coeffs = signs[0] * values[0]
        for other in range(1, COALS):
            coeffs = coeffs + signs[other] * values[other]
        shap = jnp.dot(
            weights,
            values.reshape(COALS * E_ROWS, CANDS),
            preferred_element_type=f32,
            precision=lax.Precision.HIGHEST,
        )
        return coeffs.reshape(END, R, CANDS), halves(shap)

    def halves(shap):
        shap = shap.reshape(16, 8, CANDS)
        low = lax.broadcasted_iota(jnp.int32, (16, 8, 128), 1) < 4
        return jnp.where(low, shap[:, :, :128], shap[:, :, 128:])

    def exchange(src, dst, g, kind):
        for k in FAR_FIRST:
            peer = lax.rem(c + k, COALS)
            pltpu.make_async_remote_copy(
                src_ref=src.at[g * COALS + peer],
                dst_ref=dst.at[g * COALS + c],
                send_sem=tail_send.at[kind],
                recv_sem=tail_recv.at[kind, g],
                device_id=(l, peer),
                device_id_type=MESH,
            ).start()
        dst[g * COALS + c] = src[g * COALS + c]

    def scatter(g, count):
        n = count * R
        column = jnp.sum(
            jnp.where(eye((n, 128)), logs_of(g)[0:1], 0.0), axis=1, keepdims=True
        )
        values = capped[g, pl.ds(0, n)] - column
        first = c * 64 + g * (2 * GROUP)
        shap = jnp.dot(
            shapley_weights((16 * 8, n), lambda column: first + column // 4),
            values,
            preferred_element_type=f32,
            precision=lax.Precision.HIGHEST,
        )
        values = values.reshape(count, R, CANDS)
        for h in range(2):
            send1[pl.ds(g * COALS, count), h] = values[:, :, 128 * h : 128 * h + 128]
            if count < GROUP:
                send1[pl.ds(g * COALS + count, GROUP - count), h] = jnp.zeros(
                    (GROUP - count, 8, 128), f32
                )
        send1[pl.ds(g * COALS, COALS), 2] = halves(shap)

    def gather(g):
        whole(recv1.at[pl.ds(0, 15)], tail_recv.at[1, g]).wait_recv()
        slots = pl.ds(g * COALS, COALS)
        got = recv1[slots, 0:2]
        for bit in range(4):
            step = 1 << bit
            pairs = got.reshape(COALS // (2 * step), 2, step, 2, 8, 128)
            got = jnp.concatenate(
                [pairs[:, :1], pairs[:, 1:] - pairs[:, :1]], axis=1
            ).reshape(COALS, 2, 8, 128)
        total = jnp.sum(recv1[slots, 2], axis=0)
        send2[slots, 0:2] = got
        send2[slots, 2] = jnp.broadcast_to(total[None], (COALS, 8, 128))

    away = jnp.where(x == 3, 0, jnp.where(x == 1, 2, 1)) + 3 - y
    lag = (HOP * (LAST - l) + 10 + 45 * away + 32) // 33
    lag = jnp.where(l == LAST, 0, jnp.where(l == 0, MAX_LAG, lag))

    def tick(t, carry):
        @pl.when(t < M)
        def _():
            work(t)

        @pl.when((l == 0) & (t == M))
        def _():
            turn_answers()

        b = t - lag

        @pl.when((l < LAST) & (b >= 0) & (b < M))
        def _():
            for f in range(FIN_CHUNKS):
                fin_copy(b, f, l, 0).wait_recv()
                spread(b, f)

        @pl.when(b == HALF - 1)
        def _():
            read(0, HALF, 0, 0)

        @pl.when(b == GROUP - 1)
        def _():
            read(HALF, HALF, 0, HALF * R)

        @pl.when(b == GROUP)
        def _():
            send_sums(0)

        @pl.when(b == GROUP + 6)
        def _():
            scatter(0, GROUP)

        @pl.when(b == GROUP + HALF - 1)
        def _():
            read(GROUP, HALF, 1, 0)

        @pl.when(b == GROUP + HALF)
        def _():
            exchange(send1, recv1, 0, 1)

        @pl.when(b == GROUP + HALF + 3)
        def _():
            gather(0)

        @pl.when(b == GROUP + HALF + 4)
        def _():
            exchange(send2, recv2, 0, 2)

        @pl.when(b == M - END - 1)
        def _():
            read(GROUP + HALF, HALF - END, 1, HALF * R)
            send_sums(1)

        @pl.when(b == M - 1)
        def _():
            scatter(1, GROUP - END)
            exchange(send1, recv1, 1, 1)
            read_end()

        @pl.when(b == M + 1)
        def _():
            end_logs()

        @pl.when(b == M + 2)
        def _():
            gather(1)
            exchange(send2, recv2, 1, 2)

        return carry

    lax.fori_loop(0, M + MAX_LAG + 3, tick, 0)

    end_coeffs, end_shap = end_result()

    for g in range(N_GROUPS):
        whole(recv2.at[pl.ds(0, 15)], tail_recv.at[2, g]).wait_recv()
    coeffs = jnp.concatenate([recv2[:, 0], recv2[:, 1]], axis=-1)
    coeffs = jnp.concatenate([coeffs[: M - END], end_coeffs], axis=0)
    upper = lax.broadcasted_iota(jnp.int32, (M, R, CANDS), 1) >= 4
    lower = jnp.concatenate([coeffs[:, 4:], coeffs[:, :4]], axis=1)
    coeffs = coeffs - jnp.where(upper, lower, 0.0)
    for bit in range(5):
        step = 1 << bit
        pairs = coeffs.reshape(M // (2 * step), 2, step, R, CANDS)
        coeffs = jnp.concatenate(
            [pairs[:, :1], pairs[:, 1:] - pairs[:, :1]], axis=1
        ).reshape(M, R, CANDS)
    out_ref[:, 0] = coeffs[:, :4]
    out_ref[:, 1] = coeffs[:, 4:]
    shap = jnp.sum(recv2[:, 2].reshape(N_GROUPS, COALS, 8, 128), axis=0)
    shap = (shap + end_shap)[:GROUPS]
    shap_ref[:, :, :128] = shap[:, :4]
    shap_ref[:, :, 128:] = shap[:, 4:]

    waits = [
        (sums, 15 * (N_GROUPS + 1)),
        (send1, 15 * N_GROUPS),
        (send2, 15 * N_GROUPS),
        (ends, 15),
        (lines, 15),
    ]
    for kind, (ref, count) in enumerate(waits):
        whole(ref.at[pl.ds(0, count)], tail_send.at[kind]).wait_send()

    @pl.when(l < LAST)
    def _():
        for b in range(M - DEPTH, M):
            whole(rows.at[b], chain_send.at[b % DEPTH]).wait_send()

    @pl.when(y > 1)
    def _():
        whole(fin, fin_send.at[0]).wait_send()

    @pl.when(y == 1)
    def _():
        whole(fin.at[pl.ds(0, LATE)], fin_send.at[0]).wait_send()

    @pl.when(y == 3)
    def _():
        whole(fin.at[pl.ds(LATE, M - LATE)], fin_send.at[3]).wait_send()

    @pl.when((l == 15) | (l == 11))
    def _():
        whole(fin, fin_send.at[1]).wait_send()

    @pl.when(l == 15)
    def _():
        whole(fin, fin_send.at[2]).wait_send()


def per_device(
    base_rows,
    group_out,
    pre_gain,
    w_query,
    w_key,
    w_value,
    w_out,
    post_gain,
    key_cache,
    value_cache,
    final_gain,
    answer_rows,
):
    cosine, sine = rope_rows()
    vmem = pl.BlockSpec(memory_space=pltpu.VMEM)
    hbm = pl.BlockSpec(memory_space=pl.ANY)
    exchange = pltpu.VMEM((N_GROUPS * COALS, 3, 8, 128), f32)
    coeffs, shapley = pl.pallas_call(
        kernel,
        out_shape=(
            jax.ShapeDtypeStruct((M, 2, 4, CANDS), f32),
            jax.ShapeDtypeStruct((GROUPS, 4, CANDS), f32),
        ),
        in_specs=[vmem] * 7 + [hbm] * 7,
        out_specs=(vmem, vmem),
        scratch_shapes=[
            pltpu.VMEM((D, 512), bf16),
            pltpu.VMEM((256, D), bf16),
            pltpu.VMEM((PREFIX, HEAD), bf16),
            pltpu.VMEM((HEAD, PREFIX), bf16),
            pltpu.VMEM((PREFIX, HEAD), bf16),
            pltpu.VMEM((CANDS, D), bf16),
            pltpu.VMEM((D, CANDS), bf16),
            pltpu.VMEM((GROUPS, R, D), f32),
            pltpu.VMEM((M, R, D), f32),
            pltpu.VMEM((M, R, D), f32),
            pltpu.VMEM((N_GROUPS, G_ROWS, CANDS), f32),
            pltpu.VMEM(((N_GROUPS + 1) * SECTIONS, 8, 128), f32),
            exchange,
            exchange,
            exchange,
            exchange,
            pltpu.VMEM((COALS, E_ROWS, CANDS), f32),
            pltpu.VMEM((COALS, 8, 128), f32),
            pltpu.SemaphoreType.DMA((7,)),
            pltpu.SemaphoreType.DMA((M, CHUNKS)),
            pltpu.SemaphoreType.DMA((DEPTH,)),
            pltpu.SemaphoreType.DMA((M, FIN_CHUNKS)),
            pltpu.SemaphoreType.DMA((4,)),
            pltpu.SemaphoreType.DMA((5,)),
            pltpu.SemaphoreType.DMA((3, N_GROUPS + 1)),
        ],
        compiler_params=pltpu.CompilerParams(
            collective_id=0, has_side_effects=True, vmem_limit_bytes=58 << 20
        ),
    )(
        base_rows,
        group_out,
        pre_gain,
        post_gain,
        final_gain,
        jnp.asarray(cosine),
        jnp.asarray(sine),
        w_query[0],
        w_key[0],
        w_value[0],
        w_out[0],
        key_cache[0],
        value_cache[0],
        answer_rows,
    )
    return coeffs.reshape(64, 4, CANDS), shapley


def solution(mesh):
    placed = (
        P(),
        P(),
        P("section", None),
        P("section", None, None),
        P("section", None, None),
        P("section", None, None),
        P("section", None, None),
        P("section", None),
        P("section", None, None),
        P("section", None, None),
        P(),
        P("section", None),
    )
    return jax.shard_map(
        per_device,
        mesh=mesh,
        in_specs=placed,
        out_specs=(P("coal", None, "section"), P(None, None, "section")),
        check_vma=False,
    )
```
